1024 devices in a mesh: gx: 4 (over x), gy: 16 (over z_hi, y), gz: 16 (over z_lo, core).
Axes of the slice: x: 4, y: 4, z: 32 (z_hi: 4, z_lo: 8; z = z_hi * 8 + z_lo), core: 2. Of those that a mesh axis runs over, the one named last changes fastest.
Arguments:
- inputs: bfloat16 [768, 6144], P(('gx', 'gz'), 'gy'), may hold values from -6 to 6
- cotangent: bfloat16 [768, 6144], P(('gx', 'gz'), 'gy'), may hold values from -1.1953125 to 1.1953125
- up_weight: bfloat16 [6144, 24576], P('gy', ('gz', 'gx')), may hold values from -0.078125 to 0.078125
- down_weight: bfloat16 [24576, 6144], P(('gz', 'gx'), 'gy'), may hold values from -0.0390625 to 0.0390625
Outputs:
- grad_inputs: bfloat16 [768, 6144], P(('gx', 'gz'), 'gy')
- grad_up: float32 [6144, 24576], P('gy', ('gz', 'gx'))
- grad_down: float32 [24576, 6144], P(('gz', 'gx'), 'gy')
The draws below stay inside these ranges and needn't reach their ends.
All inputs are finite; a program needn't handle non-finite values.
Results may differ from the reference program's by a relative error of at most 0.0049.
Values may be sent and summed in bfloat16 or wider, within the bound.
A program may use at most 32 MiB of HBM per device.

```python
import jax
import jax.numpy as jnp

D = 6144
FF = 24576
TOKENS = 768


def levels(rng, dims, cuts, low, top_value):
    level = 1.0
    for position, blocks in cuts:
        draws = jax.random.uniform(jax.random.fold_in(jax.random.fold_in(rng, 6), position), (blocks,), jnp.float32, low / len(cuts), top_value / len(cuts))
        level = level * jnp.repeat(jnp.exp(draws), dims[position] // blocks).reshape((-1,) + (1,) * (len(dims) - 1 - position))
    return level


def centred(key, shape, spread, most, cuts=(), dtype=jnp.bfloat16):
    array = spread * jax.random.normal(key, shape, jnp.float32)
    if cuts:
        array = array * levels(key, shape, cuts, -0.22, 0.18)
    return jnp.clip(array, -most, most).astype(dtype)


def setup_inputs(seed: int = 0) -> dict:
    key_list = jax.random.split(jax.random.key(seed), 5)
    inputs = centred(key_list[0], (TOKENS, D), 1.0, 6.0, ((0, 64), (1, 16)))
    cotangent = centred(key_list[1], (TOKENS, D), 0.2, 1.1953125, ((0, 64), (1, 16)))
    up_weight = centred(key_list[2], (D, FF), D ** -0.5, 0.078125, ((0, 16), (1, 64)))
    down_weight = centred(key_list[3], (FF, D), FF ** -0.5, 0.0390625, ((0, 64), (1, 16)))
    return dict(inputs=inputs, cotangent=cotangent, up_weight=up_weight, down_weight=down_weight)


def gelu_exact(value):
    return jax.nn.gelu(value, approximate=False)

def reference(inputs, cotangent, up_weight, down_weight):
    preact = jnp.dot(inputs, up_weight, preferred_element_type=jnp.float32)
    grad_hidden = jnp.dot(cotangent, down_weight.T, preferred_element_type=jnp.float32)
    activated, pullback = jax.vjp(gelu_exact, preact)
    grad_preact = pullback(grad_hidden)[0].astype(jnp.bfloat16)
    hidden = activated.astype(jnp.bfloat16)
    grad_down = jnp.dot(hidden.T, cotangent, preferred_element_type=jnp.float32)
    grad_up = jnp.dot(inputs.T, grad_preact, preferred_element_type=jnp.float32)
    grad_inputs = jnp.dot(grad_preact, up_weight.T, preferred_element_type=jnp.float32).astype(jnp.bfloat16)
    return (grad_inputs, grad_up, grad_down)
```

```python
import functools
import math

import jax
import jax.numpy as jnp
from jax import lax
from jax.experimental import pallas as pl
from jax.experimental.pallas import tpu as pltpu
from jax.sharding import PartitionSpec as P

MESH = pl.DeviceIdType.MESH
BF = jnp.bfloat16
F32 = jnp.float32

NK = 3
W = 384
ROWS = 256
YR = 64
ZR = 16
COPIES = 160


def dot(a, b, da, db):
    return lax.dot_general(a, b, (((da,), (db,)), ((), ())), preferred_element_type=F32)


def mod(a, n):
    return lax.rem(a + n, n)


def rev3(v):
    return lax.rem(v, 2) * 4 + lax.rem(lax.div(v, 2), 2) * 2 + lax.div(v, 4)


def kernel(
    in_ref, ct_ref, w1_ref, w2_ref, gi_ref, gu_ref, gd_ref,
    gath, xc, pf, pb, ry, ty, sf, sb, rz, tz, hg, rf, rc, xs, rx, zin, zs, rzz, send_sem, recv_sem,
):
    gx, gy, gz = lax.axis_index("gx"), lax.axis_index("gy"), lax.axis_index("gz")
    zh, y = lax.div(gy, 4), lax.rem(gy, 4)
    zl, c = lax.div(gz, 2), lax.rem(gz, 2)

    def at_x(d):
        return (mod(gx + d, 4), gy, gz)

    def at_y(d):
        return (gx, zh * 4 + mod(y + d, 4), gz)

    def at_zh(d):
        return (gx, mod(zh + d, 4) * 4 + y, gz)

    def at_zl(v):
        return (gx, gy, v * 2 + c)

    def zl_xor(m):
        return zl + m - 2 * m * lax.rem(lax.div(zl, m), 2)

    core = (gx, gy, zl * 2 + 1 - c)

    barrier = pltpu.get_barrier_semaphore()
    partners = [core, at_x(1), at_x(2), at_x(3), at_y(1), at_y(3), at_zh(1), at_zh(3)]
    partners += [at_zl(lax.rem(zl + d, 8)) for d in range(1, 8)]
    for p in partners:
        pl.semaphore_signal(barrier, inc=1, device_id=p, device_id_type=MESH)

    q = rev3(zl)
    gath[c, gx, pl.ds(pl.multiple_of(16 * q, 16), 16), :] = jnp.zeros((16, 2 * W), BF)
    row = pl.multiple_of(16 * q, 16)
    gath[c, gx, pl.ds(row, 12), 0:W] = in_ref[...]
    gath[c, gx, pl.ds(row, 12), W : 2 * W] = ct_ref[...]

    pl.semaphore_wait(barrier, len(partners))

    copies = []

    def send(src, dst, device):
        n = len(copies)
        copy = pltpu.make_async_remote_copy(
            src_ref=src, dst_ref=dst, send_sem=send_sem.at[n], recv_sem=recv_sem.at[n],
            device_id=device, device_id_type=MESH,
        )
        copy.start()
        copies.append(copy)
        return copy

    def share(ref, device):
        return send(ref, ref, device)

    def slots(xx, start, n):
        return gath.at[c, xx, pl.ds(pl.multiple_of(16 * start, 16), 16 * n), :]

    share(slots(gx, q, 1), at_zl(zl_xor(4))).wait_recv()
    share(slots(gx, lax.div(q, 2) * 2, 2), at_zl(zl_xor(2))).wait_recv()
    h = lax.div(q, 4)
    last = share(slots(gx, h * 4, 4), at_zl(zl_xor(1)))
    xl, xr, xo = mod(gx - 1, 4), mod(gx + 1, 4), mod(gx + 2, 4)
    r0 = share(slots(gx, h * 4, 4), at_x(1))
    l0 = share(slots(gx, h * 4, 4), at_x(3))
    last.wait_recv()
    r1 = share(slots(gx, (1 - h) * 4, 4), at_x(1))
    l1 = share(slots(gx, (1 - h) * 4, 4), at_x(3))
    c0 = share(gath.at[c, gx], core)
    r0.wait_recv()
    r2 = share(slots(xl, h * 4, 4), at_x(1))
    l0.wait_recv()
    l1.wait_recv()
    l2 = share(slots(xr, (1 - h) * 4, 4), at_x(3))
    c1 = share(gath.at[c, xr], core)
    r1.wait_recv()
    c2 = share(gath.at[c, xl], core)

    i = lax.broadcasted_iota(jnp.int32, (96, 128), 0)
    j = lax.broadcasted_iota(jnp.int32, (96, 128), 1)
    source = 16 * lax.div(lax.rem(i, 32), 4) + 4 * lax.div(i, 32) + lax.rem(i, 4)
    pick = jnp.where(source == j, 1.0, 0.0).astype(BF)

    def compact(cc, xx):
        rows = dot(pick, gath[cc, xx], 1, 0).astype(BF)
        at = pl.multiple_of((cc * 4 + xx) * 32, 32)
        for k in range(NK):
            xc[k, pl.ds(at, 32), :] = rows[32 * k : 32 * k + 32]

    compact(c, gx)
    compact(c, xl)
    compact(c, xr)
    c0.wait_recv()
    compact(1 - c, gx)
    r2.wait_recv()
    l2.wait_recv()
    c3 = share(gath.at[c, xo], core)
    compact(c, xo)
    c1.wait_recv()
    compact(1 - c, xr)
    c2.wait_recv()
    compact(1 - c, xl)
    c3.wait_recv()
    compact(1 - c, xo)

    def piece(ref, k, t, at, n):
        return ref.at[k, t, pl.ds(pl.multiple_of(n * at, n), n), :]

    def scatter_a(k, srcb, n, pos, to, recv):
        l1 = send(piece(srcb, k, 0, mod(pos + 2, 4), n), recv.at[k, 0], to(3))
        r1 = send(piece(srcb, k, 1, mod(pos + 2, 4), n), recv.at[k, 1], to(1))
        l2 = send(piece(srcb, k, 1, mod(pos - 1, 4), n), recv.at[k, 2], to(3))
        r2 = send(piece(srcb, k, 0, mod(pos + 1, 4), n), recv.at[k, 3], to(1))
        return l1, r1, l2, r2

    def scatter_b(k, srcf, n, pos, to, recv, tmp, first):
        l1, r1, _, _ = first
        l1.wait_recv()
        tmp[k, 0] = (piece(srcf, k, 0, mod(pos - 1, 4), n)[...] + recv[k, 0].astype(F32)).astype(BF)
        l3 = send(tmp.at[k, 0], recv.at[k, 4], to(3))
        r1.wait_recv()
        tmp[k, 1] = (piece(srcf, k, 1, mod(pos + 1, 4), n)[...] + recv[k, 1].astype(F32)).astype(BF)
        r3 = send(tmp.at[k, 1], recv.at[k, 5], to(1))
        return l3, r3

    def scatter_c(k, srcf, n, pos, recv, first, second):
        _, _, l2, r2 = first
        l3, r3 = second
        r2.wait_recv()
        l3.wait_recv()
        a = piece(srcf, k, 0, pos, n)[...] + recv[k, 3].astype(F32) + recv[k, 4].astype(F32)
        l2.wait_recv()
        r3.wait_recv()
        b = piece(srcf, k, 1, pos, n)[...] + recv[k, 2].astype(F32) + recv[k, 5].astype(F32)
        return a, b

    def rows_of(k, base, at, n):
        return pl.ds(pl.multiple_of(base + n * at, n), n)

    def gather_a(k, base, n, pos, to):
        own = hg.at[k, :, rows_of(k, base, pos, n), :]
        return share(own, to(1)), share(own, to(3))

    def gather_b(k, base, n, pos, to, first):
        r, l = first
        r.wait_recv()
        r2 = share(hg.at[k, 0, rows_of(k, base, mod(pos - 1, 4), n), :], to(1))
        l.wait_recv()
        l2 = share(hg.at[k, 1, rows_of(k, base, mod(pos + 1, 4), n), :], to(3))
        return r2, l2

    K = range(NK)
    ya, yb, za, zb, ga, gb, fa, fb = ([None] * NK for _ in range(8))
    for k in K:
        a = dot(xc[k, :, 0:W], w1_ref[...], 1, 0)
        pf[k, 0] = a
        pb[k, 0] = a.astype(BF)
        b = dot(xc[k, :, W : 2 * W], w2_ref[...], 1, 1)
        pf[k, 1] = b
        pb[k, 1] = b.astype(BF)
        ya[k] = scatter_a(k, pb, YR, y, at_y, ry)
    for k in K:
        yb[k] = scatter_b(k, pf, YR, y, at_y, ry, ty, ya[k])
    for k in K:
        a, b = scatter_c(k, pf, YR, y, ry, ya[k], yb[k])
        sf[k, 0], sf[k, 1] = a, b
        sb[k, 0], sb[k, 1] = a.astype(BF), b.astype(BF)
        za[k] = scatter_a(k, sb, ZR, zh, at_zh, rz)
    for k in K:
        zb[k] = scatter_b(k, sf, ZR, zh, at_zh, rz, tz, za[k])
    for k in K:
        pre, grad = scatter_c(k, sf, ZR, zh, rz, za[k], zb[k])
        cdf = 0.5 * (1.0 + lax.erf(pre * math.sqrt(0.5)))
        pdf = jnp.exp(-0.5 * pre * pre) * (1.0 / math.sqrt(2.0 * math.pi))
        own = rows_of(k, YR * y, zh, ZR)
        hg[k, 0, own, :] = (pre * cdf).astype(BF)
        hg[k, 1, own, :] = (grad * (cdf + pre * pdf)).astype(BF)
        ga[k] = gather_a(k, YR * y, ZR, zh, at_zh)
    for k in K:
        gb[k] = gather_b(k, YR * y, ZR, zh, at_zh, ga[k])
    for k in K:
        for copy in gb[k]:
            copy.wait_recv()
        fa[k] = gather_a(k, 0, YR, y, at_y)
    for k in K:
        fb[k] = gather_b(k, 0, YR, y, at_y, fa[k])

    cs, xsend = [None] * NK, [None] * NK
    for k in K:
        for copy in fb[k]:
            copy.wait_recv()
        rf[k] = dot(hg[k, 1], w1_ref[...], 1, 1)
        cs[k] = send(rf.at[k, pl.ds(pl.multiple_of(128 * (1 - c), 128), 128), :], rc.at[k], core)
        gu = dot(xc[k, :, 0:W], hg[k, 1], 0, 0)
        gd = dot(hg[k, 0], xc[k, :, W : 2 * W], 0, 0)
        if k == 0:
            gu_ref[...] = gu
            gd_ref[...] = gd
        else:
            gu_ref[...] += gu
            gd_ref[...] += gd
        cs[k].wait_recv()
        half = pl.ds(pl.multiple_of(128 * c, 128), 128)
        rf[k, half, :] = rf[k, half, :] + rc[k]
        xs[k] = rf[k, half, :].astype(BF)
        xsend[k] = [
            send(xs.at[k, pl.ds(pl.multiple_of(32 * mod(gx + d, 4), 32), 32), :], rx.at[k, d - 1], at_x(d))
            for d in range(1, 4)
        ]
    for k in K:
        total = rf[k, pl.ds(pl.multiple_of(128 * c + 32 * gx, 32), 32), :]
        for d in range(3):
            xsend[k][d].wait_recv()
            total += rx[k, d].astype(F32)
        zin[32 * k : 32 * k + 32, :] = total.astype(BF)
    zs[...] = dot(pick, zin[...], 0, 0).astype(BF)
    zsend = []
    for d in range(1, 8):
        to = lax.rem(zl + d, 8)
        zsend.append(send(zs.at[pl.ds(pl.multiple_of(16 * rev3(to), 16), 16), :], rzz.at[d - 1], at_zl(to)))
    total = zs[pl.ds(row, 16), :].astype(F32)
    for d in range(7):
        zsend[d].wait_recv()
        total += rzz[d].astype(F32)
    gi_ref[...] = total[0:12].astype(BF)

    for copy in copies:
        copy.wait_send()


def body(inputs, cotangent, up_weight, down_weight):
    vmem = pl.BlockSpec(memory_space=pltpu.VMEM)
    return pl.pallas_call(
        kernel,
        out_shape=(
            jax.ShapeDtypeStruct((12, W), BF),
            jax.ShapeDtypeStruct((W, W), F32),
            jax.ShapeDtypeStruct((W, W), F32),
        ),
        in_specs=[vmem] * 4,
        out_specs=(vmem,) * 3,
        scratch_shapes=[
            pltpu.VMEM((2, 4, 128, 2 * W), BF),
            pltpu.VMEM((NK, ROWS, 2 * W), BF),
            pltpu.VMEM((NK, 2, ROWS, W), F32),
            pltpu.VMEM((NK, 2, ROWS, W), BF),
            pltpu.VMEM((NK, 6, YR, W), BF),
            pltpu.VMEM((NK, 2, YR, W), BF),
            pltpu.VMEM((NK, 2, YR, W), F32),
            pltpu.VMEM((NK, 2, YR, W), BF),
            pltpu.VMEM((NK, 6, ZR, W), BF),
            pltpu.VMEM((NK, 2, ZR, W), BF),
            pltpu.VMEM((NK, 2, ROWS, W), BF),
            pltpu.VMEM((NK, ROWS, W), F32),
            pltpu.VMEM((NK, 128, W), F32),
            pltpu.VMEM((NK, 128, W), BF),
            pltpu.VMEM((NK, 3, 32, W), BF),
            pltpu.VMEM((96, W), BF),
            pltpu.VMEM((128, W), BF),
            pltpu.VMEM((7, 16, W), BF),
            pltpu.SemaphoreType.DMA((COPIES,)),
            pltpu.SemaphoreType.DMA((COPIES,)),
        ],
        compiler_params=pltpu.CompilerParams(
            collective_id=0, has_side_effects=True, vmem_limit_bytes=40 * 1024 * 1024
        ),
        name="mlp_backward",
    )(inputs, cotangent, up_weight, down_weight)


def solution(mesh):
    placed = (
        P(("gx", "gz"), "gy"),
        P(("gx", "gz"), "gy"),
        P("gy", ("gz", "gx")),
        P(("gz", "gx"), "gy"),
    )
    return jax.shard_map(
        body,
        mesh=mesh,
        in_specs=placed,
        out_specs=(P(("gx", "gz"), "gy"), P("gy", ("gz", "gx")), P(("gz", "gx"), "gy")),
        check_vma=False,
    )
```

```python
import functools
import math

import jax
import jax.numpy as jnp
from jax import lax
from jax.experimental import pallas as pl
from jax.experimental.pallas import tpu as pltpu
from jax.sharding import PartitionSpec as P

MESH = pl.DeviceIdType.MESH
BF = jnp.bfloat16
F32 = jnp.float32

NK = 3
W = 384
ROWS = 256
YR = 64
ZR = 16
COPIES = 160


def dot(a, b, da, db):
    return lax.dot_general(a, b, (((da,), (db,)), ((), ())), preferred_element_type=F32)


def mod(a, n):
    return lax.rem(a + n, n)


def rev3(v):
    return lax.rem(v, 2) * 4 + lax.rem(lax.div(v, 2), 2) * 2 + lax.div(v, 4)


def flip(v, m):
    return v + m - 2 * m * lax.rem(lax.div(v, m), 2)


def kernel(
    in_hbm, ct_hbm, w1_hbm, w2_hbm, gi_ref, gu_ref, gd_ref,
    tin, w1_ref, w2_ref, gath, xc, pf, pb, ry, ry3, ty, sf, sb, rz, tz, hg, rf, rc, rx, zin, zs, rzz,
    load_sem, send_sem, recv_sem,
):
    gx, gy, gz = lax.axis_index("gx"), lax.axis_index("gy"), lax.axis_index("gz")
    zh, y = lax.div(gy, 4), lax.rem(gy, 4)
    zl, c = lax.div(gz, 2), lax.rem(gz, 2)

    loads = [
        pltpu.make_async_copy(src, dst, load_sem.at[n])
        for n, (src, dst) in enumerate(
            [(in_hbm, tin.at[0]), (ct_hbm, tin.at[1]), (w1_hbm, w1_ref), (w2_hbm, w2_ref)]
        )
    ]
    for load in loads:
        load.start()

    def at_x(d):
        return (mod(gx + d, 4), gy, gz)

    def at_y(d):
        return (gx, zh * 4 + mod(y + d, 4), gz)

    def at_zh(d):
        return (gx, mod(zh + d, 4) * 4 + y, gz)

    def at_zl(v):
        return (gx, gy, v * 2 + c)

    core = (gx, gy, zl * 2 + 1 - c)

    barrier = pltpu.get_barrier_semaphore()
    partners = [at_zh(1), at_zh(3)]
    partners += [at_zl(lax.rem(zl + d, 8)) for d in range(1, 8)]
    partners += [at_x(1), at_x(2), at_x(3), at_y(1), at_y(3), core]
    for p in partners:
        pl.semaphore_signal(barrier, inc=1, device_id=p, device_id_type=MESH)

    q = rev3(zl)
    row = pl.multiple_of(16 * q, 16)
    gath[pl.ds(row, 16), :] = jnp.zeros((16, 2 * W), BF)
    loads[0].wait()
    gath[pl.ds(row, 12), 0:W] = tin[0]
    loads[1].wait()
    gath[pl.ds(row, 12), W : 2 * W] = tin[1]

    i = lax.broadcasted_iota(jnp.int32, (96, 128), 0)
    j = lax.broadcasted_iota(jnp.int32, (96, 128), 1)
    source = 16 * lax.div(lax.rem(i, 32), 4) + 4 * lax.div(i, 32) + lax.rem(i, 4)
    pick = jnp.where(source == j, 1.0, 0.0).astype(BF)

    pl.semaphore_wait(barrier, len(partners))

    copies = []

    def send(src, dst, device):
        n = len(copies)
        copy = pltpu.make_async_remote_copy(
            src_ref=src, dst_ref=dst, send_sem=send_sem.at[n], recv_sem=recv_sem.at[n],
            device_id=device, device_id_type=MESH,
        )
        copy.start()
        copies.append(copy)
        return copy

    def share(ref, device):
        return send(ref, ref, device)

    def slot(v):
        return gath.at[pl.ds(pl.multiple_of(16 * v, 16), 16), :]

    p4, p2, p1 = at_zl(flip(zl, 4)), at_zl(flip(zl, 2)), at_zl(flip(zl, 1))
    s4 = share(slot(q), p4)
    s2 = share(slot(q), p2)
    s1 = [share(slot(q), p1)]
    s4.wait_recv()
    s24 = share(slot(flip(q, 1)), p2)
    s1.append(share(slot(flip(q, 1)), p1))
    s2.wait_recv()
    s1.append(share(slot(flip(q, 2)), p1))
    s24.wait_recv()
    s1.append(share(slot(flip(flip(q, 2), 1)), p1))
    for copy in s1:
        copy.wait_recv()

    rows = dot(pick, gath[...], 1, 0).astype(BF)
    for t in range(3):
        xc[9 + t, c] = rows[32 * t : 32 * t + 32]

    def block(first, n=3):
        return xc.at[pl.ds(first, n), c]

    def half(unit, at):
        return xc.at[unit, c, pl.ds(at, 16), :]

    ra = send(block(9, 2), block(0, 2), at_x(1))
    lb = send(block(10, 2), block(4, 2), at_x(3))
    rb = send(block(11, 1), block(2, 1), at_x(1))
    la = send(block(9, 1), block(3, 1), at_x(3))
    c3 = share(block(9), core)
    ra.wait_recv()
    rr = [send(block(0, 1), block(6, 1), at_x(1)), send(half(1, 0), half(7, 0), at_x(1))]
    lb.wait_recv()
    ll = [send(block(5, 1), block(8, 1), at_x(3)), send(half(4, 16), half(7, 16), at_x(3))]
    rb.wait_recv()
    c0 = share(block(0), core)
    la.wait_recv()
    c1 = share(block(3), core)

    def piece(ref, k, t, at, n):
        return ref.at[k, t, pl.ds(pl.multiple_of(n * at, n), n), :]

    def scatter_a(k, srcb, n, pos, to, recv):
        l1 = send(piece(srcb, k, 0, mod(pos + 2, 4), n), recv.at[k, 0], to(3))
        r1 = send(piece(srcb, k, 1, mod(pos + 2, 4), n), recv.at[k, 1], to(1))
        l2 = send(piece(srcb, k, 1, mod(pos - 1, 4), n), recv.at[k, 2], to(3))
        r2 = send(piece(srcb, k, 0, mod(pos + 1, 4), n), recv.at[k, 3], to(1))
        return l1, r1, l2, r2

    def scatter_b(k, srcf, n, pos, to, recv, last, tmp, first):
        l1, r1, _, _ = first
        l1.wait_recv()
        tmp[k, 0] = (piece(srcf, k, 0, mod(pos - 1, 4), n)[...] + recv[k, 0].astype(F32)).astype(tmp.dtype)
        l3 = send(tmp.at[k, 0], last.at[k, 0], to(3))
        r1.wait_recv()
        tmp[k, 1] = (piece(srcf, k, 1, mod(pos + 1, 4), n)[...] + recv[k, 1].astype(F32)).astype(tmp.dtype)
        r3 = send(tmp.at[k, 1], last.at[k, 1], to(1))
        return l3, r3

    def scatter_c(k, srcf, n, pos, recv, last, first, second):
        _, _, l2, r2 = first
        l3, r3 = second
        r2.wait_recv()
        l3.wait_recv()
        a = piece(srcf, k, 0, pos, n)[...] + recv[k, 3].astype(F32) + last[k, 0].astype(F32)
        l2.wait_recv()
        r3.wait_recv()
        b = piece(srcf, k, 1, pos, n)[...] + recv[k, 2].astype(F32) + last[k, 1].astype(F32)
        return a, b

    def rows_of(base, at, n):
        return pl.ds(pl.multiple_of(base + n * at, n), n)

    def gather_a(k, base, n, pos, to):
        own = hg.at[k, :, rows_of(base, pos, n), :]
        return share(own, to(1)), share(own, to(3))

    def gather_b(k, base, n, pos, to, first):
        r, l = first
        r.wait_recv()
        r2 = share(hg.at[k, 0, rows_of(base, mod(pos - 1, 4), n), :], to(1))
        l.wait_recv()
        l2 = share(hg.at[k, 1, rows_of(base, mod(pos + 1, 4), n), :], to(3))
        return r2, l2

    ya, yb, za, zb, ga, gb, fa, fb, cs = ([None] * NK for _ in range(9))

    def tokens(k, t):
        return xc[4 * k : 4 * k + 4, :, :, W * t : W * t + W].reshape(ROWS, W)

    def products(k):
        for t, (w, dim) in enumerate(((w1_ref, 0), (w2_ref, 1))):
            a = dot(tokens(k, t), w[...], 1, dim)
            pf[k, t] = a
            pb[k, t] = a.astype(BF)

    def y_first(k):
        ya[k] = scatter_a(k, pb, YR, y, at_y, ry)

    def y_second(k):
        yb[k] = scatter_b(k, pf, YR, y, at_y, ry, ry3, ty, ya[k])

    def z_first(k):
        a, b = scatter_c(k, pf, YR, y, ry, ry3, ya[k], yb[k])
        sf[k, 0], sf[k, 1] = a, b
        sb[k, 0], sb[k, 1] = a.astype(BF), b.astype(BF)
        za[k] = scatter_a(k, sb, ZR, zh, at_zh, rz.at[:, 0:4])

    def z_second(k):
        zb[k] = scatter_b(k, sf, ZR, zh, at_zh, rz, rz.at[:, 4:6], tz, za[k])

    def z_back(k):
        pre, grad = scatter_c(k, sf, ZR, zh, rz, rz.at[:, 4:6], za[k], zb[k])
        cdf = 0.5 * (1.0 + lax.erf(pre * math.sqrt(0.5)))
        pdf = jnp.exp(-0.5 * pre * pre) * (1.0 / math.sqrt(2.0 * math.pi))
        own = rows_of(YR * y, zh, ZR)
        hg[k, 0, own, :] = (pre * cdf).astype(BF)
        hg[k, 1, own, :] = (grad * (cdf + pre * pdf)).astype(BF)
        ga[k] = gather_a(k, YR * y, ZR, zh, at_zh)

    def z_relay(k):
        gb[k] = gather_b(k, YR * y, ZR, zh, at_zh, ga[k])

    def y_back(k):
        for copy in gb[k]:
            copy.wait_recv()
        fa[k] = gather_a(k, 0, YR, y, at_y)

    def y_relay(k):
        fb[k] = gather_b(k, 0, YR, y, at_y, fa[k])

    def back_core(k):
        for copy in fb[k]:
            copy.wait_recv()
        rf[k] = dot(hg[k, 1], w1_ref[...], 1, 1).reshape(4, 2, 32, W)
        cs[k] = send(rf.at[k, :, 1 - c], rc.at[k], core)

    def back_sum(k):
        cs[k].wait_recv()
        for u in range(4):
            rf[k, u, c] = rf[k, u, c] + rc[k, u]

    def back_x(k, unit, n, at, side):
        return send(rf.at[k, pl.ds(unit, n), c], rx.at[side, pl.ds(at, n)], at_x((3, 1, 2)[side]))

    def weights(k):
        gu = dot(tokens(k, 0), hg[k, 1], 0, 0)
        gd = dot(hg[k, 0], tokens(k, 1), 0, 0)
        if k == 0:
            gu_ref[...] = gu
            gd_ref[...] = gd
        else:
            gu_ref[...] += gu
            gd_ref[...] += gd

    c3.wait_recv()
    c0.wait_recv()
    c1.wait_recv()
    loads[2].wait()
    loads[3].wait()
    products(0)
    y_first(0)
    for copy in rr + ll:
        copy.wait_recv()
    c2 = share(block(6), core)
    y_second(0)
    c2.wait_recv()
    products(1)
    y_first(1)
    products(2)
    z_first(0)
    y_second(1)
    y_first(2)
    z_first(1)
    y_second(2)
    z_second(0)
    z_first(2)
    z_second(1)
    z_back(0)
    z_second(2)
    z_back(1)
    z_relay(0)
    z_back(2)
    z_relay(1)
    y_back(0)
    z_relay(2)
    y_relay(0)
    y_back(1)
    back_core(0)
    y_relay(1)
    back_sum(0)
    xs = [back_x(0, 0, 3, 0, 0), back_x(0, 3, 1, 0, 1)]
    y_back(2)
    weights(0)
    back_core(1)
    back_sum(1)
    xs += [back_x(1, 2, 2, 0, 2), back_x(1, 0, 2, 1, 1)]
    y_relay(2)
    weights(1)
    back_core(2)
    weights(2)
    back_sum(2)
    xs.append(back_x(2, 0, 1, 2, 2))
    for copy in xs:
        copy.wait_recv()
    for t in range(3):
        total = rf[2, 1 + t, c] + rx[0, t] + rx[1, t] + rx[2, t]
        zin[32 * t : 32 * t + 32, :] = total.astype(BF)
    zs[...] = dot(pick, zin[...], 0, 0).astype(BF)
    zsend = []
    for d in (4, 3, 5, 2, 6, 1, 7):
        to = lax.rem(zl + d, 8)
        zsend.append(send(zs.at[pl.ds(pl.multiple_of(16 * rev3(to), 16), 16), :], rzz.at[d - 1], at_zl(to)))
    for copy in zsend:
        copy.wait_recv()
    total = zs[pl.ds(row, 16), :].astype(F32)
    for d in range(7):
        total += rzz[d].astype(F32)
    gi_ref[...] = total[0:12].astype(BF)

    for copy in copies:
        copy.wait_send()


def body(inputs, cotangent, up_weight, down_weight):
    vmem = pl.BlockSpec(memory_space=pltpu.VMEM)
    hbm = pl.BlockSpec(memory_space=pl.ANY)
    return pl.pallas_call(
        kernel,
        out_shape=(
            jax.ShapeDtypeStruct((12, W), BF),
            jax.ShapeDtypeStruct((W, W), F32),
            jax.ShapeDtypeStruct((W, W), F32),
        ),
        in_specs=[hbm] * 4,
        out_specs=(vmem,) * 3,
        scratch_shapes=[
            pltpu.VMEM((2, 12, W), BF),
            pltpu.VMEM((W, W), BF),
            pltpu.VMEM((W, W), BF),
            pltpu.VMEM((128, 2 * W), BF),
            pltpu.VMEM((12, 2, 32, 2 * W), BF),
            pltpu.VMEM((NK, 2, ROWS, W), F32),
            pltpu.VMEM((NK, 2, ROWS, W), BF),
            pltpu.VMEM((NK, 4, YR, W), BF),
            pltpu.VMEM((NK, 2, YR, W), F32),
            pltpu.VMEM((NK, 2, YR, W), F32),
            pltpu.VMEM((NK, 2, YR, W), F32),
            pltpu.VMEM((NK, 2, YR, W), BF),
            pltpu.VMEM((NK, 6, ZR, W), BF),
            pltpu.VMEM((NK, 2, ZR, W), BF),
            pltpu.VMEM((NK, 2, ROWS, W), BF),
            pltpu.VMEM((NK, 4, 2, 32, W), F32),
            pltpu.VMEM((NK, 4, 32, W), F32),
            pltpu.VMEM((3, 3, 32, W), F32),
            pltpu.VMEM((96, W), BF),
            pltpu.VMEM((128, W), BF),
            pltpu.VMEM((7, 16, W), BF),
            pltpu.SemaphoreType.DMA((4,)),
            pltpu.SemaphoreType.DMA((COPIES,)),
            pltpu.SemaphoreType.DMA((COPIES,)),
        ],
        compiler_params=pltpu.CompilerParams(
            collective_id=0, has_side_effects=True, vmem_limit_bytes=40 * 1024 * 1024
        ),
        name="mlp_backward",
    )(inputs, cotangent, up_weight, down_weight)


def solution(mesh):
    placed = (
        P(("gx", "gz"), "gy"),
        P(("gx", "gz"), "gy"),
        P("gy", ("gz", "gx")),
        P(("gz", "gx"), "gy"),
    )
    return jax.shard_map(
        body,
        mesh=mesh,
        in_specs=placed,
        out_specs=(P(("gx", "gz"), "gy"), P("gy", ("gz", "gx")), P(("gz", "gx"), "gy")),
        check_vma=False,
    )
```

```python
import functools
import math

import jax
import jax.numpy as jnp
from jax import lax
from jax.experimental import pallas as pl
from jax.experimental.pallas import tpu as pltpu
from jax.sharding import PartitionSpec as P

MESH = pl.DeviceIdType.MESH
BF = jnp.bfloat16
F32 = jnp.float32

NK = 3
W = 384
ROWS = 256
YR = 64
ZR = 16
COPIES = 160


def dot(a, b, da, db):
    return lax.dot_general(a, b, (((da,), (db,)), ((), ())), preferred_element_type=F32)


def mod(a, n):
    return lax.rem(a + n, n)


def rev3(v):
    return lax.rem(v, 2) * 4 + lax.rem(lax.div(v, 2), 2) * 2 + lax.div(v, 4)


def flip(v, m):
    return v + m - 2 * m * lax.rem(lax.div(v, m), 2)


def kernel(
    in_hbm, ct_hbm, w1_hbm, w2_hbm, gi_ref, gu_ref, gd_ref,
    tin, w1_ref, w2_ref, gath, xc, pf, pb, ry, ry3, ty, ry0, ty0, sf, sb, rz, tz, hg, rf, rc, rx, xs2, rx2, zin, zs, rzz,
    load_sem, send_sem, recv_sem,
):
    gx, gy, gz = lax.axis_index("gx"), lax.axis_index("gy"), lax.axis_index("gz")
    zh, y = lax.div(gy, 4), lax.rem(gy, 4)
    zl, c = lax.div(gz, 2), lax.rem(gz, 2)

    loads = [
        pltpu.make_async_copy(src, dst, load_sem.at[n])
        for n, (src, dst) in enumerate(
            [(in_hbm, tin.at[0]), (ct_hbm, tin.at[1]), (w1_hbm, w1_ref), (w2_hbm, w2_ref)]
        )
    ]
    for load in loads:
        load.start()

    def at_x(d):
        return (mod(gx + d, 4), gy, gz)

    def at_y(d):
        return (gx, zh * 4 + mod(y + d, 4), gz)

    def at_zh(d):
        return (gx, mod(zh + d, 4) * 4 + y, gz)

    def at_zl(v):
        return (gx, gy, v * 2 + c)

    core = (gx, gy, zl * 2 + 1 - c)

    barrier = pltpu.get_barrier_semaphore()
    partners = [at_zh(1), at_zh(3)]
    partners += [at_zl(lax.rem(zl + d, 8)) for d in range(1, 8)]
    partners += [at_x(1), at_x(2), at_x(3), at_y(1), at_y(3), core]
    for p in partners:
        pl.semaphore_signal(barrier, inc=1, device_id=p, device_id_type=MESH)

    q = rev3(zl)
    row = pl.multiple_of(16 * q, 16)
    gath[pl.ds(row, 16), :] = jnp.zeros((16, 2 * W), BF)
    loads[0].wait()
    gath[pl.ds(row, 12), 0:W] = tin[0]
    loads[1].wait()
    gath[pl.ds(row, 12), W : 2 * W] = tin[1]

    i = lax.broadcasted_iota(jnp.int32, (96, 128), 0)
    j = lax.broadcasted_iota(jnp.int32, (96, 128), 1)
    source = 16 * lax.div(lax.rem(i, 32), 4) + 4 * lax.div(i, 32) + lax.rem(i, 4)
    pick = jnp.where(source == j, 1.0, 0.0).astype(BF)

    pl.semaphore_wait(barrier, len(partners))

    copies = []

    def send(src, dst, device):
        n = len(copies)
        copy = pltpu.make_async_remote_copy(
            src_ref=src, dst_ref=dst, send_sem=send_sem.at[n], recv_sem=recv_sem.at[n],
            device_id=device, device_id_type=MESH,
        )
        copy.start()
        copies.append(copy)
        return copy

    def share(ref, device):
        return send(ref, ref, device)

    def slots(start, n):
        return gath.at[pl.ds(pl.multiple_of(16 * start, 16), 16 * n), :]

    share(slots(q, 1), at_zl(flip(zl, 4))).wait_recv()
    share(slots(lax.div(q, 2) * 2, 2), at_zl(flip(zl, 2))).wait_recv()
    share(slots(lax.div(q, 4) * 4, 4), at_zl(flip(zl, 1))).wait_recv()

    rows = dot(pick, gath[...], 1, 0).astype(BF)
    for t, unit in enumerate((0, 1, 11)):
        xc[unit, c] = rows[32 * t : 32 * t + 32]

    def u(unit):
        return xc.at[unit, c]

    def two(unit):
        return xc.at[pl.ds(unit, 2), c]

    def half(unit, at):
        return xc.at[unit, c, pl.ds(at, 16), :]

    r0, l0 = send(u(0), u(2), at_x(1)), send(u(0), u(3), at_x(3))
    k0 = share(two(0), core)
    r1, l1 = send(u(1), u(4), at_x(1)), send(u(1), u(5), at_x(3))
    r0.wait_recv()
    l0.wait_recv()
    k1 = share(two(2), core)
    rr0 = send(u(2), u(6), at_x(1))
    r2, l2 = send(u(11), u(8), at_x(1)), send(u(11), u(9), at_x(3))
    r1.wait_recv()
    rr1 = send(half(4, 0), half(7, 0), at_x(1))
    l1.wait_recv()
    ll1 = send(half(5, 16), half(7, 16), at_x(3))
    k2 = share(two(4), core)

    def piece(ref, k, t, at, n):
        return ref.at[k, t, pl.ds(pl.multiple_of(n * at, n), n), :]

    def scatter_a(k, srcb, n, pos, to, recv):
        l1 = send(piece(srcb, k, 0, mod(pos + 2, 4), n), recv.at[k, 0], to(3))
        r1 = send(piece(srcb, k, 1, mod(pos + 2, 4), n), recv.at[k, 1], to(1))
        l2 = send(piece(srcb, k, 1, mod(pos - 1, 4), n), recv.at[k, 2], to(3))
        r2 = send(piece(srcb, k, 0, mod(pos + 1, 4), n), recv.at[k, 3], to(1))
        return l1, r1, l2, r2

    def scatter_b(k, srcf, n, pos, to, recv, last, tmp, first):
        l1, r1, _, _ = first
        l1.wait_recv()
        tmp[k, 0] = (piece(srcf, k, 0, mod(pos - 1, 4), n)[...] + recv[k, 0].astype(F32)).astype(tmp.dtype)
        l3 = send(tmp.at[k, 0], last.at[k, 0], to(3))
        r1.wait_recv()
        tmp[k, 1] = (piece(srcf, k, 1, mod(pos + 1, 4), n)[...] + recv[k, 1].astype(F32)).astype(tmp.dtype)
        r3 = send(tmp.at[k, 1], last.at[k, 1], to(1))
        return l3, r3

    def scatter_c(k, srcf, n, pos, recv, last, first, second):
        _, _, l2, r2 = first
        l3, r3 = second
        r2.wait_recv()
        l3.wait_recv()
        a = piece(srcf, k, 0, pos, n)[...] + recv[k, 3].astype(F32) + last[k, 0].astype(F32)
        l2.wait_recv()
        r3.wait_recv()
        b = piece(srcf, k, 1, pos, n)[...] + recv[k, 2].astype(F32) + last[k, 1].astype(F32)
        return a, b

    def rows_of(base, at, n):
        return pl.ds(pl.multiple_of(base + n * at, n), n)

    def gather_a(k, t, base, n, pos, to):
        own = hg.at[k, t, rows_of(base, pos, n), :]
        return share(own, to(1)), share(own, to(3))

    ya, yb, za, zb, cs = ([None] * NK for _ in range(5))
    ga, gb, fa, fb = ([[None] * 2 for _ in range(NK)] for _ in range(4))

    def tokens(k, t):
        return xc[4 * k : 4 * k + 4, :, :, W * t : W * t + W].reshape(ROWS, W)

    def products(k):
        for t, (w, dim) in enumerate(((w1_ref, 0), (w2_ref, 1))):
            a = dot(tokens(k, t), w[...], 1, dim)
            pf[k, t] = a
            pb[k, t] = a.astype(BF)

    def y_first(k):
        ya[k] = scatter_a(k, pb, YR, y, at_y, ry)

    def y_second(k):
        yb[k] = scatter_b(k, pf, YR, y, at_y, ry, ry3 if k else ry0, ty if k else ty0, ya[k])

    def z_first(k):
        a, b = scatter_c(k, pf, YR, y, ry, ry3 if k else ry0, ya[k], yb[k])
        sf[k, 0], sf[k, 1] = a, b
        sb[k, 0], sb[k, 1] = a.astype(BF), b.astype(BF)
        za[k] = scatter_a(k, sb, ZR, zh, at_zh, rz.at[:, 0:4])

    def z_second(k):
        zb[k] = scatter_b(k, sf, ZR, zh, at_zh, rz, rz.at[:, 4:6], tz, za[k])

    def z_back(k):
        pre, grad = scatter_c(k, sf, ZR, zh, rz, rz.at[:, 4:6], za[k], zb[k])
        cdf = 0.5 * (1.0 + lax.erf(pre * math.sqrt(0.5)))
        pdf = jnp.exp(-0.5 * pre * pre) * (1.0 / math.sqrt(2.0 * math.pi))
        own = rows_of(YR * y, zh, ZR)
        hg[k, 0, own, :] = (pre * cdf).astype(BF)
        hg[k, 1, own, :] = (grad * (cdf + pre * pdf)).astype(BF)
        z_own(k, 1)

    def z_own(k, t):
        ga[k][t] = gather_a(k, t, YR * y, ZR, zh, at_zh)

    def z_relay(k, t):
        r, l = ga[k][t]
        if (k + t) % 2:
            r.wait_recv()
            gb[k][t] = share(hg.at[k, t, rows_of(YR * y, mod(zh - 1, 4), ZR), :], at_zh(1)), l
        else:
            l.wait_recv()
            gb[k][t] = share(hg.at[k, t, rows_of(YR * y, mod(zh + 1, 4), ZR), :], at_zh(3)), r

    def y_back(k, t):
        for copy in gb[k][t]:
            copy.wait_recv()
        fa[k][t] = gather_a(k, t, 0, YR, y, at_y)

    def y_relay(k, t):
        r, l = fa[k][t]
        r.wait_recv()
        r2 = share(hg.at[k, t, rows_of(YR * mod(y - 1, 4), 0, 32), :], at_y(1))
        l.wait_recv()
        l2 = share(hg.at[k, t, rows_of(YR * mod(y + 1, 4) + 32, 0, 32), :], at_y(3))
        fb[k][t] = r2, l2

    def back_core(k):
        for copy in fb[k][1]:
            copy.wait_recv()
        rf[k] = dot(hg[k, 1], w1_ref[...], 1, 1).reshape(4, 2, 32, W)
        cs[k] = send(rf.at[k, :, 1 - c], rc.at[k], core)

    def back_sum(k):
        cs[k].wait_recv()
        for u in range(4):
            rf[k, u, c] = rf[k, u, c] + rc[k, u]

    def back_x(k, unit, n, at, side):
        return send(rf.at[k, pl.ds(unit, n), c], rx.at[side, pl.ds(at, n)], at_x((3, 1, 2)[side]))

    def add(ref, k, value):
        if k == 0:
            ref[...] = value
        else:
            ref[...] += value

    def grad_up(k):
        add(gu_ref, k, dot(tokens(k, 0), hg[k, 1], 0, 0))

    def grad_down(k):
        for copy in fb[k][0]:
            copy.wait_recv()
        add(gd_ref, k, dot(hg[k, 0], tokens(k, 1), 0, 0))

    k0.wait_recv()
    k1.wait_recv()
    loads[2].wait()
    loads[3].wait()
    products(0)
    y_first(0)
    l2.wait_recv()
    ll2 = send(u(9), u(10), at_x(3))
    r2.wait_recv()
    k4 = share(two(8), core)
    k5 = share(u(11), core)
    for copy in (rr0, rr1, ll1):
        copy.wait_recv()
    k3 = share(two(6), core)
    y_second(0)
    k2.wait_recv()
    k3.wait_recv()
    products(1)
    y_first(1)
    ll2.wait_recv()
    k6 = share(u(10), core)
    z_first(0)
    for copy in (k4, k5, k6):
        copy.wait_recv()
    products(2)
    y_second(1)
    y_first(2)
    z_first(1)
    y_second(2)
    z_second(0)
    z_first(2)
    z_second(1)
    z_back(0)
    z_second(2)
    z_back(1)
    z_relay(0, 1)
    z_back(2)
    z_relay(1, 1)
    z_own(0, 0)
    y_back(0, 1)
    z_relay(2, 1)
    z_own(1, 0)
    z_own(2, 0)
    y_relay(0, 1)
    y_back(1, 1)
    back_core(0)
    z_relay(0, 0)
    y_relay(1, 1)
    back_sum(0)
    xs = [back_x(0, 2, 1, 0, 0), back_x(0, 3, 1, 0, 1)]
    grad_up(0)
    y_back(2, 1)
    back_core(1)
    back_sum(1)
    xs += [back_x(1, 2, 2, 0, 2), back_x(1, 0, 1, 1, 0), back_x(1, 1, 1, 1, 1)]
    z_relay(1, 0)
    y_relay(2, 1)
    grad_up(1)
    back_core(2)
    z_relay(2, 0)
    grad_up(2)
    back_sum(2)
    for side, unit in ((2, 2), (0, 0), (1, 1)):
        xs2[side] = rf[2, unit, c].astype(BF)
        xs.append(send(xs2.at[side], rx2.at[side], at_x((3, 1, 2)[side])))
    y_back(0, 0)
    y_back(1, 0)
    for copy in xs:
        copy.wait_recv()
    for t in range(3):
        own = (rf[0, 0, c], rf[0, 1, c], rf[2, 3, c])[t]
        for side in range(3):
            own += rx[side, t] if t < 2 else rx2[side].astype(F32)
        zin[32 * t : 32 * t + 32, :] = own.astype(BF)
    zs[...] = dot(pick, zin[...], 0, 0).astype(BF)
    zsend = []
    for d in (4, 3, 5, 2, 6, 1, 7):
        to = lax.rem(zl + d, 8)
        zsend.append(send(zs.at[pl.ds(pl.multiple_of(16 * rev3(to), 16), 16), :], rzz.at[d - 1], at_zl(to)))
    y_back(2, 0)
    y_relay(0, 0)
    y_relay(1, 0)
    grad_down(0)
    y_relay(2, 0)
    grad_down(1)
    grad_down(2)
    for copy in zsend:
        copy.wait_recv()
    total = zs[pl.ds(row, 16), :].astype(F32)
    for d in range(7):
        total += rzz[d].astype(F32)
    gi_ref[...] = total[0:12].astype(BF)

    for copy in copies:
        copy.wait_send()


def body(inputs, cotangent, up_weight, down_weight):
    vmem = pl.BlockSpec(memory_space=pltpu.VMEM)
    hbm = pl.BlockSpec(memory_space=pltpu.HBM)
    return pl.pallas_call(
        kernel,
        out_shape=(
            jax.ShapeDtypeStruct((12, W), BF),
            jax.ShapeDtypeStruct((W, W), F32),
            jax.ShapeDtypeStruct((W, W), F32),
        ),
        in_specs=[hbm] * 4,
        out_specs=(vmem,) * 3,
        scratch_shapes=[
            pltpu.VMEM((2, 12, W), BF),
            pltpu.VMEM((W, W), BF),
            pltpu.VMEM((W, W), BF),
            pltpu.VMEM((128, 2 * W), BF),
            pltpu.VMEM((12, 2, 32, 2 * W), BF),
            pltpu.VMEM((NK, 2, ROWS, W), F32),
            pltpu.VMEM((NK, 2, ROWS, W), BF),
            pltpu.VMEM((NK, 4, YR, W), BF),
            pltpu.VMEM((NK, 2, YR, W), F32),
            pltpu.VMEM((NK, 2, YR, W), F32),
            pltpu.VMEM((1, 2, YR, W), BF),
            pltpu.VMEM((1, 2, YR, W), BF),
            pltpu.VMEM((NK, 2, YR, W), F32),
            pltpu.VMEM((NK, 2, YR, W), BF),
            pltpu.VMEM((NK, 6, ZR, W), BF),
            pltpu.VMEM((NK, 2, ZR, W), BF),
            pltpu.VMEM((NK, 2, ROWS, W), BF),
            pltpu.VMEM((NK, 4, 2, 32, W), F32),
            pltpu.VMEM((NK, 4, 32, W), F32),
            pltpu.VMEM((3, 2, 32, W), F32),
            pltpu.VMEM((3, 32, W), BF),
            pltpu.VMEM((3, 32, W), BF),
            pltpu.VMEM((96, W), BF),
            pltpu.VMEM((128, W), BF),
            pltpu.VMEM((7, 16, W), BF),
            pltpu.SemaphoreType.DMA((4,)),
            pltpu.SemaphoreType.DMA((COPIES,)),
            pltpu.SemaphoreType.DMA((COPIES,)),
        ],
        compiler_params=pltpu.CompilerParams(
            collective_id=0, has_side_effects=True, vmem_limit_bytes=40 * 1024 * 1024
        ),
        name="mlp_backward",
    )(inputs, cotangent, up_weight, down_weight)


def solution(mesh):
    placed = (
        P(("gx", "gz"), "gy"),
        P(("gx", "gz"), "gy"),
        P("gy", ("gz", "gx")),
        P(("gz", "gx"), "gy"),
    )
    return jax.shard_map(
        body,
        mesh=mesh,
        in_specs=placed,
        out_specs=(P(("gx", "gz"), "gy"), P("gy", ("gz", "gx")), P(("gz", "gx"), "gy")),
        check_vma=False,
    )
```

```python
import functools
import math

import jax
import jax.numpy as jnp
from jax import lax
from jax.experimental import pallas as pl
from jax.experimental.pallas import tpu as pltpu
from jax.sharding import PartitionSpec as P

MESH = pl.DeviceIdType.MESH
BF = jnp.bfloat16
F32 = jnp.float32

NK = 3
W = 384
ROWS = 256
YR = 64
ZR = 16
COPIES = 160


def dot(a, b, da, db):
    return lax.dot_general(a, b, (((da,), (db,)), ((), ())), preferred_element_type=F32)


def mod(a, n):
    return lax.rem(a + n, n)


def rev3(v):
    return lax.rem(v, 2) * 4 + lax.rem(lax.div(v, 2), 2) * 2 + lax.div(v, 4)


def flip(v, m):
    return v + m - 2 * m * lax.rem(lax.div(v, m), 2)


def kernel(
    in_hbm, ct_hbm, w1_hbm, w2_hbm, gi_ref, gu_ref, gd_ref,
    tin, w1_ref, w2_ref, gath, xc, pf, pb, ry, ry3, ty, ry0, ty0, sf, sb, rz, tz, hg, rf, rc, rx, xs2, rx2, zin, zs, rzz, zs2, rzz2,
    load_sem, send_sem, recv_sem,
):
    gx, gy, gz = lax.axis_index("gx"), lax.axis_index("gy"), lax.axis_index("gz")
    zh, y = lax.div(gy, 4), lax.rem(gy, 4)
    zl, c = lax.div(gz, 2), lax.rem(gz, 2)

    loads = [
        pltpu.make_async_copy(src, dst, load_sem.at[n])
        for n, (src, dst) in enumerate(
            [(in_hbm, tin.at[0]), (ct_hbm, tin.at[1]), (w1_hbm, w1_ref), (w2_hbm, w2_ref)]
        )
    ]
    for load in loads:
        load.start()

    def at_x(d):
        return (mod(gx + d, 4), gy, gz)

    def at_y(d):
        return (gx, zh * 4 + mod(y + d, 4), gz)

    def at_zh(d):
        return (gx, mod(zh + d, 4) * 4 + y, gz)

    def at_zl(v):
        return (gx, gy, v * 2 + c)

    core = (gx, gy, zl * 2 + 1 - c)

    barrier = pltpu.get_barrier_semaphore()
    partners = [at_zh(1), at_zh(3)]
    partners += [at_zl(lax.rem(zl + d, 8)) for d in range(1, 8)]
    partners += [at_x(1), at_x(2), at_x(3), at_y(1), at_y(3), core]
    for p in partners:
        pl.semaphore_signal(barrier, inc=1, device_id=p, device_id_type=MESH)

    q = rev3(zl)
    row = pl.multiple_of(16 * q, 16)
    gath[pl.ds(row, 16), :] = jnp.zeros((16, 2 * W), BF)
    loads[0].wait()
    gath[pl.ds(row, 12), 0:W] = tin[0]
    loads[1].wait()
    gath[pl.ds(row, 12), W : 2 * W] = tin[1]

    i = lax.broadcasted_iota(jnp.int32, (96, 128), 0)
    j = lax.broadcasted_iota(jnp.int32, (96, 128), 1)
    source = 16 * lax.div(lax.rem(i, 32), 4) + 4 * lax.div(i, 32) + lax.rem(i, 4)
    pick = jnp.where(source == j, 1.0, 0.0).astype(BF)

    i = lax.broadcasted_iota(jnp.int32, (192, 256), 0)
    j = lax.broadcasted_iota(jnp.int32, (192, 256), 1)
    target = 32 * lax.div(lax.rem(i, 32), 4) + 8 * lax.div(i, 64) + 4 * lax.rem(lax.div(i, 32), 2) + lax.rem(i, 4)
    pick2 = jnp.where(target == j, 1.0, 0.0).astype(BF)

    pl.semaphore_wait(barrier, len(partners))

    copies = []

    def send(src, dst, device):
        n = len(copies)
        copy = pltpu.make_async_remote_copy(
            src_ref=src, dst_ref=dst, send_sem=send_sem.at[n], recv_sem=recv_sem.at[n],
            device_id=device, device_id_type=MESH,
        )
        copy.start()
        copies.append(copy)
        return copy

    def share(ref, device):
        return send(ref, ref, device)

    def slot(v):
        return gath.at[pl.ds(pl.multiple_of(16 * v, 16), 16), :]

    p4, p2, p1 = at_zl(flip(zl, 4)), at_zl(flip(zl, 2)), at_zl(flip(zl, 1))
    s4 = share(slot(q), p4)
    s2 = share(slot(q), p2)
    s1 = [share(slot(q), p1)]
    s4.wait_recv()
    s24 = share(slot(flip(q, 1)), p2)
    s1.append(share(slot(flip(q, 1)), p1))
    s2.wait_recv()
    s1.append(share(slot(flip(q, 2)), p1))
    s24.wait_recv()
    s1.append(share(slot(flip(flip(q, 2), 1)), p1))
    for copy in s1:
        copy.wait_recv()

    rows = dot(pick, gath[...], 1, 0).astype(BF)
    for t, unit in enumerate((0, 1, 11)):
        xc[unit, c] = rows[32 * t : 32 * t + 32]

    def u(unit):
        return xc.at[unit, c]

    def two(unit):
        return xc.at[pl.ds(unit, 2), c]

    def half(unit, at):
        return xc.at[unit, c, pl.ds(at, 16), :]

    r0, l0 = send(u(0), u(2), at_x(1)), send(u(0), u(3), at_x(3))
    k0 = share(two(0), core)
    r1, l1 = send(u(1), u(4), at_x(1)), send(u(1), u(5), at_x(3))
    r0.wait_recv()
    l0.wait_recv()
    k1 = share(two(2), core)
    rr0 = send(u(2), u(6), at_x(1))
    r2, l2 = send(u(11), u(8), at_x(1)), send(u(11), u(9), at_x(3))
    r1.wait_recv()
    rr1 = send(half(4, 0), half(7, 0), at_x(1))
    l1.wait_recv()
    ll1 = send(half(5, 16), half(7, 16), at_x(3))
    k2 = share(two(4), core)

    def piece(ref, k, t, at, n):
        return ref.at[k, t, pl.ds(pl.multiple_of(n * at, n), n), :]

    def scatter_a(k, srcb, n, pos, to, recv):
        l1 = send(piece(srcb, k, 0, mod(pos + 2, 4), n), recv.at[k, 0], to(3))
        r1 = send(piece(srcb, k, 1, mod(pos + 2, 4), n), recv.at[k, 1], to(1))
        l2 = send(piece(srcb, k, 1, mod(pos - 1, 4), n), recv.at[k, 2], to(3))
        r2 = send(piece(srcb, k, 0, mod(pos + 1, 4), n), recv.at[k, 3], to(1))
        return l1, r1, l2, r2

    def scatter_b(k, srcf, n, pos, to, recv, last, tmp, first):
        l1, r1, _, _ = first
        l1.wait_recv()
        tmp[k, 0] = (piece(srcf, k, 0, mod(pos - 1, 4), n)[...] + recv[k, 0].astype(F32)).astype(tmp.dtype)
        l3 = send(tmp.at[k, 0], last.at[k, 0], to(3))
        r1.wait_recv()
        tmp[k, 1] = (piece(srcf, k, 1, mod(pos + 1, 4), n)[...] + recv[k, 1].astype(F32)).astype(tmp.dtype)
        r3 = send(tmp.at[k, 1], last.at[k, 1], to(1))
        return l3, r3

    def scatter_c(k, srcf, n, pos, recv, last, first, second):
        _, _, l2, r2 = first
        l3, r3 = second
        r2.wait_recv()
        l3.wait_recv()
        a = piece(srcf, k, 0, pos, n)[...] + recv[k, 3].astype(F32) + last[k, 0].astype(F32)
        l2.wait_recv()
        r3.wait_recv()
        b = piece(srcf, k, 1, pos, n)[...] + recv[k, 2].astype(F32) + last[k, 1].astype(F32)
        return a, b

    def rows_of(base, at, n):
        return pl.ds(pl.multiple_of(base + n * at, n), n)

    def gather_a(k, t, base, n, pos, to):
        own = hg.at[k, t, rows_of(base, pos, n), :]
        return share(own, to(1)), share(own, to(3))

    ya, yb, za, zb, cs = ([None] * NK for _ in range(5))
    ga, gb, fa, fb = ([[None] * 2 for _ in range(NK)] for _ in range(4))

    def tokens(k, t):
        return xc[4 * k : 4 * k + 4, :, :, W * t : W * t + W].reshape(ROWS, W)

    def products(k):
        for t, (w, dim) in enumerate(((w1_ref, 0), (w2_ref, 1))):
            a = dot(tokens(k, t), w[...], 1, dim)
            pf[k, t] = a
            pb[k, t] = a.astype(BF)

    def y_first(k):
        ya[k] = scatter_a(k, pb, YR, y, at_y, ry)

    def y_second(k):
        yb[k] = scatter_b(k, pf, YR, y, at_y, ry, ry3 if k else ry0, ty if k else ty0, ya[k])

    def z_first(k):
        a, b = scatter_c(k, pf, YR, y, ry, ry3 if k else ry0, ya[k], yb[k])
        sf[k, 0], sf[k, 1] = a, b
        sb[k, 0], sb[k, 1] = a.astype(BF), b.astype(BF)
        za[k] = scatter_a(k, sb, ZR, zh, at_zh, rz.at[:, 0:4])

    def z_second(k):
        zb[k] = scatter_b(k, sf, ZR, zh, at_zh, rz, rz.at[:, 4:6], tz, za[k])

    def z_back(k):
        pre, grad = scatter_c(k, sf, ZR, zh, rz, rz.at[:, 4:6], za[k], zb[k])
        cdf = 0.5 * (1.0 + lax.erf(pre * math.sqrt(0.5)))
        pdf = jnp.exp(-0.5 * pre * pre) * (1.0 / math.sqrt(2.0 * math.pi))
        own = rows_of(YR * y, zh, ZR)
        hg[k, 0, own, :] = (pre * cdf).astype(BF)
        hg[k, 1, own, :] = (grad * (cdf + pre * pdf)).astype(BF)
        z_own(k, 1)

    def z_own(k, t):
        ga[k][t] = gather_a(k, t, YR * y, ZR, zh, at_zh)

    def z_relay(k, t):
        r, l = ga[k][t]
        if (k + t) % 2:
            r.wait_recv()
            gb[k][t] = share(hg.at[k, t, rows_of(YR * y, mod(zh - 1, 4), ZR), :], at_zh(1)), l
        else:
            l.wait_recv()
            gb[k][t] = share(hg.at[k, t, rows_of(YR * y, mod(zh + 1, 4), ZR), :], at_zh(3)), r

    def y_back(k, t):
        for copy in gb[k][t]:
            copy.wait_recv()
        fa[k][t] = gather_a(k, t, 0, YR, y, at_y)

    def y_relay(k, t):
        r, l = fa[k][t]
        r.wait_recv()
        r2 = share(hg.at[k, t, rows_of(YR * mod(y - 1, 4), 0, 32), :], at_y(1))
        l.wait_recv()
        l2 = share(hg.at[k, t, rows_of(YR * mod(y + 1, 4) + 32, 0, 32), :], at_y(3))
        fb[k][t] = r2, l2

    def back_core(k):
        for copy in fb[k][1]:
            copy.wait_recv()
        rf[k] = dot(hg[k, 1], w1_ref[...], 1, 1).reshape(4, 2, 32, W)
        cs[k] = send(rf.at[k, :, 1 - c], rc.at[k], core)

    def back_sum(k):
        cs[k].wait_recv()
        for u in range(4):
            rf[k, u, c] = rf[k, u, c] + rc[k, u]

    def back_x(k, unit, n, at, side):
        return send(rf.at[k, pl.ds(unit, n), c], rx.at[side, pl.ds(at, n)], at_x((3, 1, 2)[side]))

    def add(ref, k, value):
        if k == 0:
            ref[...] = value
        else:
            ref[...] += value

    def grad_up(k):
        add(gu_ref, k, dot(tokens(k, 0), hg[k, 1], 0, 0))

    def grad_down(k):
        for copy in fb[k][0]:
            copy.wait_recv()
        add(gd_ref, k, dot(hg[k, 0], tokens(k, 1), 0, 0))

    k0.wait_recv()
    k1.wait_recv()
    loads[2].wait()
    loads[3].wait()
    products(0)
    y_first(0)
    l2.wait_recv()
    ll2 = send(u(9), u(10), at_x(3))
    r2.wait_recv()
    k4 = share(two(8), core)
    k5 = share(u(11), core)
    for copy in (rr0, rr1, ll1):
        copy.wait_recv()
    k3 = share(two(6), core)
    y_second(0)
    k2.wait_recv()
    k3.wait_recv()
    products(1)
    y_first(1)
    ll2.wait_recv()
    k6 = share(u(10), core)
    z_first(0)
    for copy in (k4, k5, k6):
        copy.wait_recv()
    products(2)
    y_second(1)
    y_first(2)
    z_first(1)
    y_second(2)
    z_second(0)
    z_first(2)
    z_second(1)
    z_back(0)
    z_second(2)
    z_back(1)
    z_relay(0, 1)
    z_back(2)
    z_relay(1, 1)
    z_own(0, 0)
    y_back(0, 1)
    z_relay(2, 1)
    z_own(1, 0)
    y_relay(0, 1)
    y_back(1, 1)
    z_relay(0, 0)
    z_own(2, 0)
    y_relay(1, 1)
    back_core(0)
    y_back(2, 1)
    back_sum(0)
    xs = [back_x(0, 2, 1, 0, 0), back_x(0, 3, 1, 0, 1)]
    back_core(1)
    y_relay(2, 1)
    back_sum(1)
    xs += [back_x(1, 2, 2, 0, 2), back_x(1, 0, 1, 1, 0), back_x(1, 1, 1, 1, 1)]
    grad_up(0)
    back_core(2)
    z_relay(1, 0)
    z_relay(2, 0)
    grad_up(1)
    back_sum(2)
    last = []
    for side, unit in ((2, 2), (0, 0), (1, 1)):
        xs2[side] = rf[2, unit, c].astype(BF)
        last.append(send(xs2.at[side], rx2.at[side], at_x((3, 1, 2)[side])))

    def over_zl(parts, spread, n, held, recv):
        for l in range(3):
            for t, part in enumerate(parts):
                at = 32 * (len(parts) * l + t)
                zin[at : at + 32, :] = part[:, 128 * l : 128 * l + 128].astype(BF)
        used = 96 * len(parts)
        held[...] = dot(spread, zin[0:used, :], 0, 0).astype(BF)
        done = []
        for d in (4, 3, 5, 2, 6, 1, 7):
            to = lax.rem(zl + d, 8)
            done.append(send(held.at[pl.ds(pl.multiple_of(n * rev3(to), n), n), :], recv.at[d - 1], at_zl(to)))
        return done

    def over_zl_sum(n, held, recv):
        total = held[pl.ds(pl.multiple_of(n * q, n), n), :].astype(F32)
        for d in range(7):
            total += recv[d].astype(F32)
        return total

    for copy in xs:
        copy.wait_recv()
    early = over_zl([rf[0, t, c] + rx[0, t] + rx[1, t] + rx[2, t] for t in range(2)], pick2, 32, zs, rzz)
    y_back(0, 0)
    y_back(1, 0)
    grad_up(2)
    for copy in last:
        copy.wait_recv()
    own = rf[2, 3, c]
    for side in range(3):
        own += rx2[side].astype(F32)
    late = over_zl([own], pick, 16, zs2, rzz2)
    y_back(2, 0)
    y_relay(0, 0)
    y_relay(1, 0)
    grad_down(0)
    y_relay(2, 0)
    grad_down(1)
    grad_down(2)
    for copy in early:
        copy.wait_recv()
    total = over_zl_sum(32, zs, rzz)
    for copy in late:
        copy.wait_recv()
    total2 = over_zl_sum(16, zs2, rzz2).astype(BF)
    i = lax.broadcasted_iota(jnp.int32, (16, 16), 0)
    j = lax.broadcasted_iota(jnp.int32, (16, 16), 1)
    for l in range(3):
        back = jnp.where((i < 4) & (j == i + 4 * l), 1.0, 0.0).astype(BF)
        columns = slice(128 * l, 128 * l + 128)
        gi_ref[0:8, columns] = total[8 * l : 8 * l + 8].astype(BF)
        gi_ref[8:12, columns] = dot(back, total2, 1, 0)[0:4].astype(BF)

    for copy in copies:
        copy.wait_send()


def body(inputs, cotangent, up_weight, down_weight):
    vmem = pl.BlockSpec(memory_space=pltpu.VMEM)
    hbm = pl.BlockSpec(memory_space=pltpu.HBM)
    return pl.pallas_call(
        kernel,
        out_shape=(
            jax.ShapeDtypeStruct((12, W), BF),
            jax.ShapeDtypeStruct((W, W), F32),
            jax.ShapeDtypeStruct((W, W), F32),
        ),
        in_specs=[hbm] * 4,
        out_specs=(vmem,) * 3,
        scratch_shapes=[
            pltpu.VMEM((2, 12, W), BF),
            pltpu.VMEM((W, W), BF),
            pltpu.VMEM((W, W), BF),
            pltpu.VMEM((128, 2 * W), BF),
            pltpu.VMEM((12, 2, 32, 2 * W), BF),
            pltpu.VMEM((NK, 2, ROWS, W), F32),
            pltpu.VMEM((NK, 2, ROWS, W), BF),
            pltpu.VMEM((NK, 4, YR, W), BF),
            pltpu.VMEM((NK, 2, YR, W), F32),
            pltpu.VMEM((NK, 2, YR, W), F32),
            pltpu.VMEM((1, 2, YR, W), BF),
            pltpu.VMEM((1, 2, YR, W), BF),
            pltpu.VMEM((NK, 2, YR, W), F32),
            pltpu.VMEM((NK, 2, YR, W), BF),
            pltpu.VMEM((NK, 6, ZR, W), BF),
            pltpu.VMEM((NK, 2, ZR, W), BF),
            pltpu.VMEM((NK, 2, ROWS, W), BF),
            pltpu.VMEM((NK, 4, 2, 32, W), F32),
            pltpu.VMEM((NK, 4, 32, W), F32),
            pltpu.VMEM((3, 2, 32, W), F32),
            pltpu.VMEM((3, 32, W), BF),
            pltpu.VMEM((3, 32, W), BF),
            pltpu.VMEM((192, 128), BF),
            pltpu.VMEM((256, 128), BF),
            pltpu.VMEM((7, 32, 128), BF),
            pltpu.VMEM((128, 128), BF),
            pltpu.VMEM((7, 16, 128), BF),
            pltpu.SemaphoreType.DMA((4,)),
            pltpu.SemaphoreType.DMA((COPIES,)),
            pltpu.SemaphoreType.DMA((COPIES,)),
        ],
        compiler_params=pltpu.CompilerParams(
            collective_id=0, has_side_effects=True, vmem_limit_bytes=56 * 1024 * 1024
        ),
        name="mlp_backward",
    )(inputs, cotangent, up_weight, down_weight)


def solution(mesh):
    placed = (
        P(("gx", "gz"), "gy"),
        P(("gx", "gz"), "gy"),
        P("gy", ("gz", "gx")),
        P(("gz", "gx"), "gy"),
    )
    return jax.shard_map(
        body,
        mesh=mesh,
        in_specs=placed,
        out_specs=(P(("gx", "gz"), "gy"), P("gy", ("gz", "gx")), P(("gz", "gx"), "gy")),
        check_vma=False,
    )
```

```python
import functools
import math

import jax
import jax.numpy as jnp
from jax import lax
from jax.experimental import pallas as pl
from jax.experimental.pallas import tpu as pltpu
from jax.sharding import PartitionSpec as P

MESH = pl.DeviceIdType.MESH
BF = jnp.bfloat16
F32 = jnp.float32

NK = 3
W = 384
ROWS = 256
YR = 64
ZR = 16
COPIES = 160


def dot(a, b, da, db):
    return lax.dot_general(a, b, (((da,), (db,)), ((), ())), preferred_element_type=F32)


def mod(a, n):
    return lax.rem(a + n, n)


def rev3(v):
    return lax.rem(v, 2) * 4 + lax.rem(lax.div(v, 2), 2) * 2 + lax.div(v, 4)


def flip(v, m):
    return v + m - 2 * m * lax.rem(lax.div(v, m), 2)


def kernel(
    in_hbm, ct_hbm, w1_hbm, w2_hbm, gi_ref, gu_hbm, gd_hbm,
    gu_ref, gd_ref, tin, w1_ref, w2_ref, gath, xc, pf, pb, ry, ry3, ty, ry0, ty0, sf, sb, rz, tz, hg, rf, rc, rx, xs2, rx2, zin, zs, rzz, zs2, rzz2,
    load_sem, store_sem, send_sem, recv_sem,
):
    gx, gy, gz = lax.axis_index("gx"), lax.axis_index("gy"), lax.axis_index("gz")
    zh, y = lax.div(gy, 4), lax.rem(gy, 4)
    zl, c = lax.div(gz, 2), lax.rem(gz, 2)

    loads = [
        pltpu.make_async_copy(src, dst, load_sem.at[n])
        for n, (src, dst) in enumerate(
            [(in_hbm, tin.at[0]), (ct_hbm, tin.at[1]), (w1_hbm, w1_ref), (w2_hbm, w2_ref)]
        )
    ]
    for load in loads:
        load.start()

    def at_x(d):
        return (mod(gx + d, 4), gy, gz)

    def at_y(d):
        return (gx, zh * 4 + mod(y + d, 4), gz)

    def at_zh(d):
        return (gx, mod(zh + d, 4) * 4 + y, gz)

    def at_zl(v):
        return (gx, gy, v * 2 + c)

    core = (gx, gy, zl * 2 + 1 - c)

    barrier = pltpu.get_barrier_semaphore()
    partners = [at_zh(1), at_zh(3)]
    partners += [at_zl(lax.rem(zl + d, 8)) for d in range(1, 8)]
    partners += [at_x(1), at_x(2), at_x(3), at_y(1), at_y(2), at_y(3), core]
    for p in partners:
        pl.semaphore_signal(barrier, inc=1, device_id=p, device_id_type=MESH)

    q = rev3(zl)
    row = pl.multiple_of(16 * q, 16)
    gath[pl.ds(row, 16), :] = jnp.zeros((16, 2 * W), BF)
    loads[0].wait()
    gath[pl.ds(row, 12), 0:W] = tin[0]
    loads[1].wait()
    gath[pl.ds(row, 12), W : 2 * W] = tin[1]

    i = lax.broadcasted_iota(jnp.int32, (96, 128), 0)
    j = lax.broadcasted_iota(jnp.int32, (96, 128), 1)
    source = 16 * lax.div(lax.rem(i, 32), 4) + 4 * lax.div(i, 32) + lax.rem(i, 4)
    pick = jnp.where(source == j, 1.0, 0.0).astype(BF)

    i = lax.broadcasted_iota(jnp.int32, (192, 256), 0)
    j = lax.broadcasted_iota(jnp.int32, (192, 256), 1)
    target = 32 * lax.div(lax.rem(i, 32), 4) + 8 * lax.div(i, 64) + 4 * lax.rem(lax.div(i, 32), 2) + lax.rem(i, 4)
    pick2 = jnp.where(target == j, 1.0, 0.0).astype(BF)

    pl.semaphore_wait(barrier, len(partners))

    copies = []

    def send(src, dst, device):
        n = len(copies)
        copy = pltpu.make_async_remote_copy(
            src_ref=src, dst_ref=dst, send_sem=send_sem.at[n], recv_sem=recv_sem.at[n],
            device_id=device, device_id_type=MESH,
        )
        copy.start()
        copies.append(copy)
        return copy

    def share(ref, device):
        return send(ref, ref, device)

    def slot(v):
        return gath.at[pl.ds(pl.multiple_of(16 * v, 16), 16), :]

    p4, p2, p1 = at_zl(flip(zl, 4)), at_zl(flip(zl, 2)), at_zl(flip(zl, 1))
    s4 = share(slot(q), p4)
    s2 = share(slot(q), p2)
    s1 = [share(slot(q), p1)]
    s4.wait_recv()
    s24 = share(slot(flip(q, 1)), p2)
    s1.append(share(slot(flip(q, 1)), p1))
    s2.wait_recv()
    s1.append(share(slot(flip(q, 2)), p1))
    s24.wait_recv()
    s1.append(share(slot(flip(flip(q, 2), 1)), p1))
    for copy in s1:
        copy.wait_recv()

    rows = dot(pick, gath[...], 1, 0).astype(BF)
    for t, unit in enumerate((0, 1, 11)):
        xc[unit, c] = rows[32 * t : 32 * t + 32]

    def u(unit):
        return xc.at[unit, c]

    def two(unit):
        return xc.at[pl.ds(unit, 2), c]

    def half(unit, at):
        return xc.at[unit, c, pl.ds(at, 16), :]

    r0, l0 = send(u(0), u(2), at_x(1)), send(u(0), u(3), at_x(3))
    k0 = share(two(0), core)
    r1, l1 = send(u(1), u(4), at_x(1)), send(u(1), u(5), at_x(3))
    r0.wait_recv()
    l0.wait_recv()
    k1 = share(two(2), core)
    rr0 = send(u(2), u(6), at_x(1))
    r2, l2 = send(u(11), u(8), at_x(1)), send(u(11), u(9), at_x(3))
    r1.wait_recv()
    rr1 = send(half(4, 0), half(7, 0), at_x(1))
    l1.wait_recv()
    ll1 = send(half(5, 16), half(7, 16), at_x(3))
    k2 = share(two(4), core)

    def piece(ref, k, t, at, n):
        return ref.at[k, t, pl.ds(pl.multiple_of(n * at, n), n), :]

    def scatter_a(k, srcb, n, pos, to, recv):
        l1 = send(piece(srcb, k, 0, mod(pos + 2, 4), n), recv.at[k, 0], to(3))
        r1 = send(piece(srcb, k, 1, mod(pos + 2, 4), n), recv.at[k, 1], to(1))
        l2 = send(piece(srcb, k, 1, mod(pos - 1, 4), n), recv.at[k, 2], to(3))
        r2 = send(piece(srcb, k, 0, mod(pos + 1, 4), n), recv.at[k, 3], to(1))
        return l1, r1, l2, r2

    def scatter_b(k, srcf, n, pos, to, recv, last, tmp, first):
        l1, r1, _, _ = first
        l1.wait_recv()
        tmp[k, 0] = (piece(srcf, k, 0, mod(pos - 1, 4), n)[...] + recv[k, 0].astype(F32)).astype(tmp.dtype)
        l3 = send(tmp.at[k, 0], last.at[k, 0], to(3))
        r1.wait_recv()
        tmp[k, 1] = (piece(srcf, k, 1, mod(pos + 1, 4), n)[...] + recv[k, 1].astype(F32)).astype(tmp.dtype)
        r3 = send(tmp.at[k, 1], last.at[k, 1], to(1))
        return l3, r3

    def scatter_c(k, srcf, n, pos, recv, last, first, second):
        _, _, l2, r2 = first
        l3, r3 = second
        r2.wait_recv()
        l3.wait_recv()
        a = piece(srcf, k, 0, pos, n)[...] + recv[k, 3].astype(F32) + last[k, 0].astype(F32)
        l2.wait_recv()
        r3.wait_recv()
        b = piece(srcf, k, 1, pos, n)[...] + recv[k, 2].astype(F32) + last[k, 1].astype(F32)
        return a, b

    def rows_of(base, at, n):
        return pl.ds(pl.multiple_of(base + n * at, n), n)

    def gather_a(k, t, base, n, pos, to):
        own = hg.at[k, t, rows_of(base, pos, n), :]
        return share(own, to(1)), share(own, to(3))

    ya, yb, za, zb, cs = ([None] * NK for _ in range(5))
    ga, gb, fa, fb = ([[None] * 2 for _ in range(NK)] for _ in range(4))

    def tokens(k, t):
        return xc[4 * k : 4 * k + 4, :, :, W * t : W * t + W].reshape(ROWS, W)

    def products(k):
        for t, (w, dim) in enumerate(((w1_ref, 0), (w2_ref, 1))):
            a = dot(tokens(k, t), w[...], 1, dim)
            pf[k, t] = a
            pb[k, t] = a.astype(BF)

    def y_first(k):
        ya[k] = scatter_a(k, pb, YR, y, at_y, ry)

    def y_second(k):
        yb[k] = scatter_b(k, pf, YR, y, at_y, ry, ry3 if k else ry0, ty if k else ty0, ya[k])

    def z_first(k):
        a, b = scatter_c(k, pf, YR, y, ry, ry3 if k else ry0, ya[k], yb[k])
        sf[k, 0], sf[k, 1] = a, b
        sb[k, 0], sb[k, 1] = a.astype(BF), b.astype(BF)
        za[k] = scatter_a(k, sb, ZR, zh, at_zh, rz.at[:, 0:4])

    def z_second(k):
        zb[k] = scatter_b(k, sf, ZR, zh, at_zh, rz, rz.at[:, 4:6], tz, za[k])

    def z_back(k):
        pre, grad = scatter_c(k, sf, ZR, zh, rz, rz.at[:, 4:6], za[k], zb[k])
        cdf = 0.5 * (1.0 + lax.erf(pre * math.sqrt(0.5)))
        pdf = jnp.exp(-0.5 * pre * pre) * (1.0 / math.sqrt(2.0 * math.pi))
        own = rows_of(YR * y, zh, ZR)
        hg[k, 0, own, :] = (pre * cdf).astype(BF)
        hg[k, 1, own, :] = (grad * (cdf + pre * pdf)).astype(BF)
        z_own(k, 1)

    def z_own(k, t):
        ga[k][t] = gather_a(k, t, YR * y, ZR, zh, at_zh)

    def z_relay(k, t):
        r, l = ga[k][t]
        if (k + t) % 2:
            r.wait_recv()
            gb[k][t] = share(hg.at[k, t, rows_of(YR * y, mod(zh - 1, 4), ZR), :], at_zh(1)), l
        else:
            l.wait_recv()
            gb[k][t] = share(hg.at[k, t, rows_of(YR * y, mod(zh + 1, 4), ZR), :], at_zh(3)), r

    def y_back(k, t):
        for copy in gb[k][t]:
            copy.wait_recv()
        fa[k][t] = gather_a(k, t, 0, YR, y, at_y)

    def y_direct(k, t):
        for copy in gb[k][t]:
            copy.wait_recv()
        own = hg.at[k, t, rows_of(0, y, YR), :]
        fb[k][t] = [share(own, at_y(d)) for d in (2, 1, 3)]

    def y_relay(k, t):
        r, l = fa[k][t]
        r.wait_recv()
        r2 = share(hg.at[k, t, rows_of(YR * mod(y - 1, 4), 0, 32), :], at_y(1))
        l.wait_recv()
        l2 = share(hg.at[k, t, rows_of(YR * mod(y + 1, 4) + 32, 0, 32), :], at_y(3))
        fb[k][t] = r2, l2

    def back_core(k):
        for copy in fb[k][1]:
            copy.wait_recv()
        rf[k] = dot(hg[k, 1], w1_ref[...], 1, 1).reshape(4, 2, 32, W)
        cs[k] = send(rf.at[k, :, 1 - c], rc.at[k], core)

    def back_sum(k):
        cs[k].wait_recv()
        for u in range(4):
            rf[k, u, c] = rf[k, u, c] + rc[k, u]

    def back_x(k, unit, n, at, side):
        return send(rf.at[k, pl.ds(unit, n), c], rx.at[side, pl.ds(at, n)], at_x((3, 1, 2)[side]))

    def back_x_short(slot, k, unit, side):
        xs2[slot] = rf[k, unit, c].astype(BF)
        return send(xs2.at[slot], rx2.at[slot], at_x((3, 1, 2)[side]))

    def add(ref, k, value):
        if k == 0:
            ref[...] = value
        else:
            ref[...] += value

    def grad_up(k):
        add(gu_ref, k, dot(tokens(k, 0), hg[k, 1], 0, 0))

    def grad_down(k):
        for copy in fb[k][0]:
            copy.wait_recv()
        add(gd_ref, k, dot(hg[k, 0], tokens(k, 1), 0, 0))

    k0.wait_recv()
    k1.wait_recv()
    loads[2].wait()
    loads[3].wait()
    products(0)
    y_first(0)
    l2.wait_recv()
    ll2 = send(u(9), u(10), at_x(3))
    r2.wait_recv()
    k4 = share(two(8), core)
    k5 = share(u(11), core)
    for copy in (rr0, rr1, ll1):
        copy.wait_recv()
    k3 = share(two(6), core)
    y_second(0)
    k2.wait_recv()
    k3.wait_recv()
    products(1)
    y_first(1)
    ll2.wait_recv()
    k6 = share(u(10), core)
    z_first(0)
    for copy in (k4, k5, k6):
        copy.wait_recv()
    products(2)
    y_second(1)
    y_first(2)
    z_first(1)
    y_second(2)
    z_second(0)
    z_first(2)
    z_second(1)
    z_back(0)
    z_second(2)
    z_back(1)
    z_relay(0, 1)
    z_back(2)
    z_relay(1, 1)
    z_own(0, 0)
    y_back(0, 1)
    z_relay(2, 1)
    z_own(1, 0)
    y_relay(0, 1)
    y_back(1, 1)
    z_own(2, 0)
    back_core(0)
    z_relay(0, 0)
    y_relay(1, 1)
    back_sum(0)
    xs = [back_x(0, 2, 1, 0, 0), back_x(0, 3, 1, 0, 1)]
    y_direct(2, 1)
    back_core(1)
    grad_up(0)
    back_sum(1)
    xs += [back_x_short(3, 1, 2, 2), back_x_short(4, 1, 3, 2), back_x(1, 0, 1, 1, 0), back_x(1, 1, 1, 1, 1)]
    z_relay(1, 0)
    z_relay(2, 0)
    back_core(2)
    y_back(0, 0)
    grad_up(1)
    back_sum(2)
    last = [back_x_short(side, 2, unit, side) for side, unit in ((2, 2), (0, 0), (1, 1))]

    def over_zl(parts, spread, n, held, recv):
        for l in range(3):
            for t, part in enumerate(parts):
                at = 32 * (len(parts) * l + t)
                zin[at : at + 32, :] = part[:, 128 * l : 128 * l + 128].astype(BF)
        used = 96 * len(parts)
        held[...] = dot(spread, zin[0:used, :], 0, 0).astype(BF)
        done = []
        for d in (4, 3, 5, 2, 6, 1, 7):
            to = lax.rem(zl + d, 8)
            done.append(send(held.at[pl.ds(pl.multiple_of(n * rev3(to), n), n), :], recv.at[d - 1], at_zl(to)))
        return done

    def over_zl_sum(n, held, recv):
        total = held[pl.ds(pl.multiple_of(n * q, n), n), :].astype(F32)
        for d in range(7):
            total += recv[d].astype(F32)
        return total

    for copy in xs:
        copy.wait_recv()
    early = over_zl([rf[0, t, c] + rx[0, t] + rx[1, t] + rx2[3 + t].astype(F32) for t in range(2)], pick2, 32, zs, rzz)
    y_relay(0, 0)
    y_back(1, 0)
    grad_up(2)
    stores = [pltpu.make_async_copy(gu_ref, gu_hbm, store_sem.at[0])]
    stores[0].start()
    for copy in last:
        copy.wait_recv()
    own = rf[2, 3, c]
    for side in range(3):
        own += rx2[side].astype(F32)
    late = over_zl([own], pick, 16, zs2, rzz2)
    y_direct(2, 0)
    y_relay(1, 0)
    grad_down(0)
    grad_down(1)
    grad_down(2)
    stores.append(pltpu.make_async_copy(gd_ref, gd_hbm, store_sem.at[1]))
    stores[1].start()
    for copy in early:
        copy.wait_recv()
    total = over_zl_sum(32, zs, rzz)
    for copy in late:
        copy.wait_recv()
    total2 = over_zl_sum(16, zs2, rzz2).astype(BF)
    i = lax.broadcasted_iota(jnp.int32, (16, 16), 0)
    j = lax.broadcasted_iota(jnp.int32, (16, 16), 1)
    for l in range(3):
        back = jnp.where((i < 4) & (j == i + 4 * l), 1.0, 0.0).astype(BF)
        columns = slice(128 * l, 128 * l + 128)
        gi_ref[0:8, columns] = total[8 * l : 8 * l + 8].astype(BF)
        gi_ref[8:12, columns] = dot(back, total2, 1, 0)[0:4].astype(BF)

    for store in stores:
        store.wait()
    for copy in copies:
        copy.wait_send()


def body(inputs, cotangent, up_weight, down_weight):
    vmem = pl.BlockSpec(memory_space=pltpu.VMEM)
    hbm = pl.BlockSpec(memory_space=pltpu.HBM)
    return pl.pallas_call(
        kernel,
        out_shape=(
            jax.ShapeDtypeStruct((12, W), BF),
            jax.ShapeDtypeStruct((W, W), F32),
            jax.ShapeDtypeStruct((W, W), F32),
        ),
        in_specs=[hbm] * 4,
        out_specs=(vmem, hbm, hbm),
        scratch_shapes=[
            pltpu.VMEM((W, W), F32),
            pltpu.VMEM((W, W), F32),
            pltpu.VMEM((2, 12, W), BF),
            pltpu.VMEM((W, W), BF),
            pltpu.VMEM((W, W), BF),
            pltpu.VMEM((128, 2 * W), BF),
            pltpu.VMEM((12, 2, 32, 2 * W), BF),
            pltpu.VMEM((NK, 2, ROWS, W), F32),
            pltpu.VMEM((NK, 2, ROWS, W), BF),
            pltpu.VMEM((NK, 4, YR, W), BF),
            pltpu.VMEM((NK, 2, YR, W), F32),
            pltpu.VMEM((NK, 2, YR, W), F32),
            pltpu.VMEM((1, 2, YR, W), BF),
            pltpu.VMEM((1, 2, YR, W), BF),
            pltpu.VMEM((NK, 2, YR, W), F32),
            pltpu.VMEM((NK, 2, YR, W), BF),
            pltpu.VMEM((NK, 6, ZR, W), BF),
            pltpu.VMEM((NK, 2, ZR, W), BF),
            pltpu.VMEM((NK, 2, ROWS, W), BF),
            pltpu.VMEM((NK, 4, 2, 32, W), F32),
            pltpu.VMEM((NK, 4, 32, W), F32),
            pltpu.VMEM((2, 2, 32, W), F32),
            pltpu.VMEM((5, 32, W), BF),
            pltpu.VMEM((5, 32, W), BF),
            pltpu.VMEM((192, 128), BF),
            pltpu.VMEM((256, 128), BF),
            pltpu.VMEM((7, 32, 128), BF),
            pltpu.VMEM((128, 128), BF),
            pltpu.VMEM((7, 16, 128), BF),
            pltpu.SemaphoreType.DMA((4,)),
            pltpu.SemaphoreType.DMA((2,)),
            pltpu.SemaphoreType.DMA((COPIES,)),
            pltpu.SemaphoreType.DMA((COPIES,)),
        ],
        compiler_params=pltpu.CompilerParams(
            collective_id=0, has_side_effects=True, vmem_limit_bytes=56 * 1024 * 1024
        ),
        name="mlp_backward",
    )(inputs, cotangent, up_weight, down_weight)


def solution(mesh):
    placed = (
        P(("gx", "gz"), "gy"),
        P(("gx", "gz"), "gy"),
        P("gy", ("gz", "gx")),
        P(("gz", "gx"), "gy"),
    )
    return jax.shard_map(
        body,
        mesh=mesh,
        in_specs=placed,
        out_specs=(P(("gx", "gz"), "gy"), P("gy", ("gz", "gx")), P(("gz", "gx"), "gy")),
        check_vma=False,
    )
```

```python
import functools
import math

import jax
import jax.numpy as jnp
from jax import lax
from jax.experimental import pallas as pl
from jax.experimental.pallas import tpu as pltpu
from jax.sharding import PartitionSpec as P

MESH = pl.DeviceIdType.MESH
BF = jnp.bfloat16
F32 = jnp.float32

NK = 3
W = 384
ROWS = 256
YR = 64
ZR = 16
COPIES = 160


def dot(a, b, da, db):
    return lax.dot_general(a, b, (((da,), (db,)), ((), ())), preferred_element_type=F32)


def mod(a, n):
    return lax.rem(a + n, n)


def rev3(v):
    return lax.rem(v, 2) * 4 + lax.rem(lax.div(v, 2), 2) * 2 + lax.div(v, 4)


def flip(v, m):
    return v + m - 2 * m * lax.rem(lax.div(v, m), 2)


def kernel(
    in_hbm, ct_hbm, w1_hbm, w2_hbm, gi_ref, gu_hbm, gd_hbm,
    gu_ref, gd_ref, tin, w1_ref, w2_ref, gath, xc, pf, pb, ry, ry3, ty, ry0, ty0, sf, sb, rz, tz, hg, rf, rc, rx, xs2, rx2, zin, zs, rzz, zs2, rzz2,
    load_sem, store_sem, send_sem, recv_sem,
):
    gx, gy, gz = lax.axis_index("gx"), lax.axis_index("gy"), lax.axis_index("gz")
    zh, y = lax.div(gy, 4), lax.rem(gy, 4)
    zl, c = lax.div(gz, 2), lax.rem(gz, 2)

    loads = [
        pltpu.make_async_copy(src, dst, load_sem.at[n])
        for n, (src, dst) in enumerate(
            [(in_hbm, tin.at[0]), (ct_hbm, tin.at[1]), (w1_hbm, w1_ref), (w2_hbm, w2_ref)]
        )
    ]
    for load in loads:
        load.start()

    def at_x(d):
        return (mod(gx + d, 4), gy, gz)

    def at_y(d):
        return (gx, zh * 4 + mod(y + d, 4), gz)

    def at_zh(d):
        return (gx, mod(zh + d, 4) * 4 + y, gz)

    def at_zl(v):
        return (gx, gy, v * 2 + c)

    core = (gx, gy, zl * 2 + 1 - c)

    barrier = pltpu.get_barrier_semaphore()
    partners = [at_zh(1), at_zh(3)]
    partners += [at_zl(lax.rem(zl + d, 8)) for d in range(1, 8)]
    partners += [at_x(1), at_x(2), at_x(3), at_y(1), at_y(2), at_y(3), core]
    for p in partners:
        pl.semaphore_signal(barrier, inc=1, device_id=p, device_id_type=MESH)

    q = rev3(zl)
    row = pl.multiple_of(16 * q, 16)
    gath[pl.ds(row, 16), :] = jnp.zeros((16, 2 * W), BF)
    loads[0].wait()
    gath[pl.ds(row, 12), 0:W] = tin[0]
    loads[1].wait()
    gath[pl.ds(row, 12), W : 2 * W] = tin[1]

    i = lax.broadcasted_iota(jnp.int32, (96, 128), 0)
    j = lax.broadcasted_iota(jnp.int32, (96, 128), 1)
    source = 16 * lax.div(lax.rem(i, 32), 4) + 4 * lax.div(i, 32) + lax.rem(i, 4)
    pick = jnp.where(source == j, 1.0, 0.0).astype(BF)

    i = lax.broadcasted_iota(jnp.int32, (192, 256), 0)
    j = lax.broadcasted_iota(jnp.int32, (192, 256), 1)
    target = 32 * lax.div(lax.rem(i, 32), 4) + 8 * lax.div(i, 64) + 4 * lax.rem(lax.div(i, 32), 2) + lax.rem(i, 4)
    pick2 = jnp.where(target == j, 1.0, 0.0).astype(BF)

    pl.semaphore_wait(barrier, len(partners))

    copies = []

    def send(src, dst, device):
        n = len(copies)
        copy = pltpu.make_async_remote_copy(
            src_ref=src, dst_ref=dst, send_sem=send_sem.at[n], recv_sem=recv_sem.at[n],
            device_id=device, device_id_type=MESH,
        )
        copy.start()
        copies.append(copy)
        return copy

    def share(ref, device):
        return send(ref, ref, device)

    def slot(v):
        return gath.at[pl.ds(pl.multiple_of(16 * v, 16), 16), :]

    p4, p2, p1 = at_zl(flip(zl, 4)), at_zl(flip(zl, 2)), at_zl(flip(zl, 1))
    s4 = share(slot(q), p4)
    s2 = share(slot(q), p2)
    s1 = [share(slot(q), p1)]
    s4.wait_recv()
    s24 = share(slot(flip(q, 1)), p2)
    s1.append(share(slot(flip(q, 1)), p1))
    s2.wait_recv()
    s1.append(share(slot(flip(q, 2)), p1))
    s24.wait_recv()
    s1.append(share(slot(flip(flip(q, 2), 1)), p1))
    for copy in s1:
        copy.wait_recv()

    rows = dot(pick, gath[...], 1, 0).astype(BF)
    for t, unit in enumerate((0, 1, 11)):
        xc[unit, c] = rows[32 * t : 32 * t + 32]

    def u(unit):
        return xc.at[unit, c]

    def two(unit):
        return xc.at[pl.ds(unit, 2), c]

    def half(unit, at):
        return xc.at[unit, c, pl.ds(at, 16), :]

    r0, l0 = send(u(0), u(2), at_x(1)), send(u(0), u(3), at_x(3))
    k0 = share(two(0), core)
    r1, l1 = send(u(1), u(4), at_x(1)), send(u(1), u(5), at_x(3))
    r0.wait_recv()
    l0.wait_recv()
    k1 = share(two(2), core)
    rr0 = send(u(2), u(6), at_x(1))
    r2, l2 = send(u(11), u(8), at_x(1)), send(u(11), u(9), at_x(3))
    r1.wait_recv()
    rr1 = send(half(4, 0), half(7, 0), at_x(1))
    l1.wait_recv()
    ll1 = send(half(5, 16), half(7, 16), at_x(3))
    k2 = share(two(4), core)

    def piece(ref, k, t, at, n):
        return ref.at[k, t, pl.ds(pl.multiple_of(n * at, n), n), :]

    def scatter_a(k, srcb, n, pos, to, recv):
        l1 = send(piece(srcb, k, 0, mod(pos + 2, 4), n), recv.at[k, 0], to(3))
        r1 = send(piece(srcb, k, 1, mod(pos + 2, 4), n), recv.at[k, 1], to(1))
        l2 = send(piece(srcb, k, 1, mod(pos - 1, 4), n), recv.at[k, 2], to(3))
        r2 = send(piece(srcb, k, 0, mod(pos + 1, 4), n), recv.at[k, 3], to(1))
        return l1, r1, l2, r2

    def scatter_b(k, srcf, n, pos, to, recv, last, tmp, first):
        l1, r1, _, _ = first
        l1.wait_recv()
        tmp[k, 0] = (piece(srcf, k, 0, mod(pos - 1, 4), n)[...] + recv[k, 0].astype(F32)).astype(tmp.dtype)
        l3 = send(tmp.at[k, 0], last.at[k, 0], to(3))
        r1.wait_recv()
        tmp[k, 1] = (piece(srcf, k, 1, mod(pos + 1, 4), n)[...] + recv[k, 1].astype(F32)).astype(tmp.dtype)
        r3 = send(tmp.at[k, 1], last.at[k, 1], to(1))
        return l3, r3

    def scatter_c(k, srcf, n, pos, recv, last, first, second):
        _, _, l2, r2 = first
        l3, r3 = second
        r2.wait_recv()
        l3.wait_recv()
        a = piece(srcf, k, 0, pos, n)[...] + recv[k, 3].astype(F32) + last[k, 0].astype(F32)
        l2.wait_recv()
        r3.wait_recv()
        b = piece(srcf, k, 1, pos, n)[...] + recv[k, 2].astype(F32) + last[k, 1].astype(F32)
        return a, b

    def rows_of(base, at, n):
        return pl.ds(pl.multiple_of(base + n * at, n), n)

    def gather_a(k, t, base, n, pos, to):
        own = hg.at[k, t, rows_of(base, pos, n), :]
        return share(own, to(1)), share(own, to(3))

    ya, yb, za, zb, cs = ([None] * NK for _ in range(5))
    ga, gb, fa, fb = ([[None] * 2 for _ in range(NK)] for _ in range(4))

    def tokens(k, t):
        return xc[4 * k : 4 * k + 4, :, :, W * t : W * t + W].reshape(ROWS, W)

    def products(k):
        for t, (w, dim) in enumerate(((w1_ref, 0), (w2_ref, 1))):
            a = dot(tokens(k, t), w[...], 1, dim)
            pf[k, t] = a
            pb[k, t] = a.astype(BF)

    def y_first(k):
        ya[k] = scatter_a(k, pb, YR, y, at_y, ry)

    def y_second(k):
        yb[k] = scatter_b(k, pf, YR, y, at_y, ry, ry3 if k else ry0, ty if k else ty0, ya[k])

    def z_first(k):
        a, b = scatter_c(k, pf, YR, y, ry, ry3 if k else ry0, ya[k], yb[k])
        sf[k, 0], sf[k, 1] = a, b
        sb[k, 0], sb[k, 1] = a.astype(BF), b.astype(BF)
        za[k] = scatter_a(k, sb, ZR, zh, at_zh, rz.at[:, 0:4])

    def z_second(k):
        zb[k] = scatter_b(k, sf, ZR, zh, at_zh, rz, rz.at[:, 4:6], tz, za[k])

    def z_back(k):
        pre, grad = scatter_c(k, sf, ZR, zh, rz, rz.at[:, 4:6], za[k], zb[k])
        cdf = 0.5 * (1.0 + lax.erf(pre * math.sqrt(0.5)))
        pdf = jnp.exp(-0.5 * pre * pre) * (1.0 / math.sqrt(2.0 * math.pi))
        own = rows_of(YR * y, zh, ZR)
        hg[k, 0, own, :] = (pre * cdf).astype(BF)
        hg[k, 1, own, :] = (grad * (cdf + pre * pdf)).astype(BF)
        z_own(k, 1)

    def z_own(k, t):
        ga[k][t] = gather_a(k, t, YR * y, ZR, zh, at_zh)

    def z_relay(k, t):
        r, l = ga[k][t]
        if (k + t) % 2:
            r.wait_recv()
            gb[k][t] = share(hg.at[k, t, rows_of(YR * y, mod(zh - 1, 4), ZR), :], at_zh(1)), l
        else:
            l.wait_recv()
            gb[k][t] = share(hg.at[k, t, rows_of(YR * y, mod(zh + 1, 4), ZR), :], at_zh(3)), r

    def y_back(k, t):
        for copy in gb[k][t]:
            copy.wait_recv()
        fa[k][t] = gather_a(k, t, 0, YR, y, at_y)

    def y_direct(k, t):
        for copy in gb[k][t]:
            copy.wait_recv()
        own = hg.at[k, t, rows_of(0, y, YR), :]
        fb[k][t] = [share(own, at_y(d)) for d in (2, 1, 3)]

    def y_relay(k, t):
        r, l = fa[k][t]
        r.wait_recv()
        r2 = share(hg.at[k, t, rows_of(YR * mod(y - 1, 4), 0, 32), :], at_y(1))
        l.wait_recv()
        l2 = share(hg.at[k, t, rows_of(YR * mod(y + 1, 4) + 32, 0, 32), :], at_y(3))
        fb[k][t] = r2, l2

    def back_core(k):
        for copy in fb[k][1]:
            copy.wait_recv()
        rf[k] = dot(hg[k, 1], w1_ref[...], 1, 1).reshape(4, 2, 32, W)
        cs[k] = send(rf.at[k, :, 1 - c], rc.at[k], core)

    def back_sum(k):
        cs[k].wait_recv()
        for u in range(4):
            rf[k, u, c] = rf[k, u, c] + rc[k, u]

    def back_x(k, unit, n, at, side):
        return send(rf.at[k, pl.ds(unit, n), c], rx.at[side, pl.ds(at, n)], at_x((3, 1, 2)[side]))

    def back_x_short(slot, k, unit, side):
        xs2[slot] = rf[k, unit, c].astype(BF)
        return send(xs2.at[slot], rx2.at[slot], at_x((3, 1, 2)[side]))

    def add(ref, k, value):
        if k == 0:
            ref[...] = value
        else:
            ref[...] += value

    def grad_up(k):
        add(gu_ref, k, dot(tokens(k, 0), hg[k, 1], 0, 0))

    def grad_down(k):
        for copy in fb[k][0]:
            copy.wait_recv()
        add(gd_ref, k, dot(hg[k, 0], tokens(k, 1), 0, 0))

    k0.wait_recv()
    k1.wait_recv()
    loads[2].wait()
    loads[3].wait()
    products(0)
    y_first(0)
    l2.wait_recv()
    ll2 = send(u(9), u(10), at_x(3))
    r2.wait_recv()
    k4 = share(two(8), core)
    k5 = share(u(11), core)
    for copy in (rr0, rr1, ll1):
        copy.wait_recv()
    k3 = share(two(6), core)
    y_second(0)
    k2.wait_recv()
    k3.wait_recv()
    products(1)
    y_first(1)
    ll2.wait_recv()
    k6 = share(u(10), core)
    z_first(0)
    for copy in (k4, k5, k6):
        copy.wait_recv()
    products(2)
    y_second(1)
    y_first(2)
    z_first(1)
    y_second(2)
    z_second(0)
    z_first(2)
    z_second(1)
    z_back(0)
    z_second(2)
    z_back(1)
    z_relay(0, 1)
    z_back(2)
    z_relay(1, 1)
    z_own(0, 0)
    y_back(0, 1)
    z_relay(2, 1)
    z_own(1, 0)
    y_relay(0, 1)
    y_back(1, 1)
    z_own(2, 0)
    back_core(0)
    z_relay(0, 0)
    y_relay(1, 1)
    back_sum(0)
    xs = [back_x(0, 2, 1, 0, 0), back_x(0, 3, 1, 0, 1)]
    y_direct(2, 1)
    back_core(1)
    grad_up(0)
    back_sum(1)
    xs += [back_x_short(3, 1, 2, 2), back_x_short(4, 1, 3, 2), back_x(1, 0, 1, 1, 0), back_x(1, 1, 1, 1, 1)]
    z_relay(1, 0)
    z_relay(2, 0)
    back_core(2)
    y_back(0, 0)
    grad_up(1)
    back_sum(2)
    last = [back_x_short(side, 2, unit, side) for side, unit in ((2, 2), (0, 0), (1, 1))]

    def over_zl(parts, spread, n, held, recv):
        for l in range(3):
            for t, part in enumerate(parts):
                at = 32 * (len(parts) * l + t)
                zin[at : at + 32, :] = part[:, 128 * l : 128 * l + 128].astype(BF)
        used = 96 * len(parts)
        held[...] = dot(spread, zin[0:used, :], 0, 0).astype(BF)
        done = []
        for d in (4, 3, 5, 2, 6, 1, 7):
            to = lax.rem(zl + d, 8)
            done.append(send(held.at[pl.ds(pl.multiple_of(n * rev3(to), n), n), :], recv.at[d - 1], at_zl(to)))
        return done

    def over_zl_sum(n, held, recv):
        total = held[pl.ds(pl.multiple_of(n * q, n), n), :].astype(F32)
        for d in range(7):
            total += recv[d].astype(F32)
        return total

    for copy in xs:
        copy.wait_recv()
    early = over_zl([rf[0, t, c] + rx[0, t] + rx[1, t] + rx2[3 + t].astype(F32) for t in range(2)], pick2, 32, zs, rzz)
    y_relay(0, 0)
    y_back(1, 0)
    grad_up(2)
    stores = [pltpu.make_async_copy(gu_ref, gu_hbm, store_sem.at[0])]
    stores[0].start()
    for copy in last:
        copy.wait_recv()
    own = rf[2, 3, c]
    for side in range(3):
        own += rx2[side].astype(F32)
    late = over_zl([own], pick, 16, zs2, rzz2)
    y_direct(2, 0)
    y_relay(1, 0)
    grad_down(0)
    grad_down(1)
    grad_down(2)
    stores.append(pltpu.make_async_copy(gd_ref, gd_hbm, store_sem.at[1]))
    stores[1].start()
    for copy in early:
        copy.wait_recv()
    total = over_zl_sum(32, zs, rzz)
    for copy in late:
        copy.wait_recv()
    total2 = over_zl_sum(16, zs2, rzz2).astype(BF)
    i = lax.broadcasted_iota(jnp.int32, (16, 16), 0)
    j = lax.broadcasted_iota(jnp.int32, (16, 16), 1)
    for l in range(3):
        back = jnp.where((i < 4) & (j == i + 4 * l), 1.0, 0.0).astype(BF)
        columns = slice(128 * l, 128 * l + 128)
        gi_ref[0:8, columns] = total[8 * l : 8 * l + 8].astype(BF)
        gi_ref[8:12, columns] = dot(back, total2, 1, 0)[0:4].astype(BF)

    for store in stores:
        store.wait()
    for copy in copies:
        copy.wait_send()


def move(a, b, c, to_a, to_b, to_c, sem):
    copies = [pltpu.make_async_copy(*refs, sem.at[n]) for n, refs in enumerate(((b, to_b), (c, to_c), (a, to_a)))]
    for copy in copies:
        copy.start()
    for copy in copies:
        copy.wait()


def body(inputs, cotangent, up_weight, down_weight):
    vmem = pl.BlockSpec(memory_space=pltpu.VMEM)
    hbm = pl.BlockSpec(memory_space=pltpu.HBM)
    results = pl.pallas_call(
        kernel,
        out_shape=(
            jax.ShapeDtypeStruct((12, W), BF),
            jax.ShapeDtypeStruct((W, W), F32),
            jax.ShapeDtypeStruct((W, W), F32),
        ),
        in_specs=[hbm] * 4,
        out_specs=(vmem, hbm, hbm),
        scratch_shapes=[
            pltpu.VMEM((W, W), F32),
            pltpu.VMEM((W, W), F32),
            pltpu.VMEM((2, 12, W), BF),
            pltpu.VMEM((W, W), BF),
            pltpu.VMEM((W, W), BF),
            pltpu.VMEM((128, 2 * W), BF),
            pltpu.VMEM((12, 2, 32, 2 * W), BF),
            pltpu.VMEM((NK, 2, ROWS, W), F32),
            pltpu.VMEM((NK, 2, ROWS, W), BF),
            pltpu.VMEM((NK, 4, YR, W), BF),
            pltpu.VMEM((NK, 2, YR, W), F32),
            pltpu.VMEM((NK, 2, YR, W), F32),
            pltpu.VMEM((1, 2, YR, W), BF),
            pltpu.VMEM((1, 2, YR, W), BF),
            pltpu.VMEM((NK, 2, YR, W), F32),
            pltpu.VMEM((NK, 2, YR, W), BF),
            pltpu.VMEM((NK, 6, ZR, W), BF),
            pltpu.VMEM((NK, 2, ZR, W), BF),
            pltpu.VMEM((NK, 2, ROWS, W), BF),
            pltpu.VMEM((NK, 4, 2, 32, W), F32),
            pltpu.VMEM((NK, 4, 32, W), F32),
            pltpu.VMEM((2, 2, 32, W), F32),
            pltpu.VMEM((5, 32, W), BF),
            pltpu.VMEM((5, 32, W), BF),
            pltpu.VMEM((192, 128), BF),
            pltpu.VMEM((256, 128), BF),
            pltpu.VMEM((7, 32, 128), BF),
            pltpu.VMEM((128, 128), BF),
            pltpu.VMEM((7, 16, 128), BF),
            pltpu.SemaphoreType.DMA((4,)),
            pltpu.SemaphoreType.DMA((2,)),
            pltpu.SemaphoreType.DMA((COPIES,)),
            pltpu.SemaphoreType.DMA((COPIES,)),
        ],
        compiler_params=pltpu.CompilerParams(
            collective_id=0, has_side_effects=True, vmem_limit_bytes=56 * 1024 * 1024
        ),
        name="mlp_backward",
    )(inputs, cotangent, up_weight, down_weight)
    return pl.pallas_call(
        move,
        out_shape=tuple(jax.ShapeDtypeStruct(r.shape, r.dtype) for r in results),
        in_specs=[hbm] * 3,
        out_specs=(hbm,) * 3,
        scratch_shapes=[pltpu.SemaphoreType.DMA((3,))],
        compiler_params=pltpu.CompilerParams(vmem_limit_bytes=56 * 1024 * 1024),
        name="move_results",
    )(*results)


def solution(mesh):
    placed = (
        P(("gx", "gz"), "gy"),
        P(("gx", "gz"), "gy"),
        P("gy", ("gz", "gx")),
        P(("gz", "gx"), "gy"),
    )
    return jax.shard_map(
        body,
        mesh=mesh,
        in_specs=placed,
        out_specs=(P(("gx", "gz"), "gy"), P("gy", ("gz", "gx")), P(("gz", "gx"), "gy")),
        check_vma=False,
    )
```

```python
import functools
import math

import jax
import jax.numpy as jnp
from jax import lax
from jax.experimental import pallas as pl
from jax.experimental.pallas import tpu as pltpu
from jax.sharding import PartitionSpec as P

MESH = pl.DeviceIdType.MESH
BF = jnp.bfloat16
F32 = jnp.float32

NK = 3
W = 384
ROWS = 256
YR = 64
ZR = 16
COPIES = 160


def dot(a, b, da, db):
    return lax.dot_general(a, b, (((da,), (db,)), ((), ())), preferred_element_type=F32)


def mod(a, n):
    return lax.rem(a + n, n)


def rev3(v):
    return lax.rem(v, 2) * 4 + lax.rem(lax.div(v, 2), 2) * 2 + lax.div(v, 4)


def flip(v, m):
    return v + m - 2 * m * lax.rem(lax.div(v, m), 2)


def kernel(
    in_hbm, ct_hbm, w1_hbm, w2_hbm, gi_ref, gu_hbm, gd_hbm,
    gu_ref, gd_ref, tin, w1_ref, w2_ref, gath, xc, pf, pb, ry, ry3, ty, ry0, ty0, sf, sb, rz, tz, hg, rf, rc, rx, xs2, rx2, zin, zs, rzz, zs2, rzz2,
    load_sem, store_sem, send_sem, recv_sem,
):
    gx, gy, gz = lax.axis_index("gx"), lax.axis_index("gy"), lax.axis_index("gz")
    zh, y = lax.div(gy, 4), lax.rem(gy, 4)
    zl, c = lax.div(gz, 2), lax.rem(gz, 2)

    loads = [
        pltpu.make_async_copy(src, dst, load_sem.at[n])
        for n, (src, dst) in enumerate(
            [(in_hbm, tin.at[0]), (ct_hbm, tin.at[1]), (w1_hbm, w1_ref), (w2_hbm, w2_ref)]
        )
    ]
    for load in loads:
        load.start()

    def at_x(d):
        return (mod(gx + d, 4), gy, gz)

    def at_y(d):
        return (gx, zh * 4 + mod(y + d, 4), gz)

    def at_zh(d):
        return (gx, mod(zh + d, 4) * 4 + y, gz)

    def at_zl(v):
        return (gx, gy, v * 2 + c)

    core = (gx, gy, zl * 2 + 1 - c)

    barrier = pltpu.get_barrier_semaphore()
    partners = [at_zh(1), at_zh(3)]
    partners += [at_zl(lax.rem(zl + d, 8)) for d in range(1, 8)]
    partners += [at_x(1), at_x(2), at_x(3), at_y(1), at_y(2), at_y(3), core]
    for p in partners:
        pl.semaphore_signal(barrier, inc=1, device_id=p, device_id_type=MESH)

    q = rev3(zl)
    row = pl.multiple_of(16 * q, 16)
    gath[pl.ds(row, 16), :] = jnp.zeros((16, 2 * W), BF)
    loads[0].wait()
    gath[pl.ds(row, 12), 0:W] = tin[0]
    loads[1].wait()
    gath[pl.ds(row, 12), W : 2 * W] = tin[1]

    i = lax.broadcasted_iota(jnp.int32, (96, 128), 0)
    j = lax.broadcasted_iota(jnp.int32, (96, 128), 1)
    source = 16 * lax.div(lax.rem(i, 32), 4) + 4 * lax.div(i, 32) + lax.rem(i, 4)
    pick = jnp.where(source == j, 1.0, 0.0).astype(BF)

    i = lax.broadcasted_iota(jnp.int32, (192, 256), 0)
    j = lax.broadcasted_iota(jnp.int32, (192, 256), 1)
    target = 32 * lax.div(lax.rem(i, 32), 4) + 8 * lax.div(i, 64) + 4 * lax.rem(lax.div(i, 32), 2) + lax.rem(i, 4)
    pick2 = jnp.where(target == j, 1.0, 0.0).astype(BF)

    pl.semaphore_wait(barrier, len(partners))

    copies = []

    def send(src, dst, device):
        n = len(copies)
        copy = pltpu.make_async_remote_copy(
            src_ref=src, dst_ref=dst, send_sem=send_sem.at[n], recv_sem=recv_sem.at[n],
            device_id=device, device_id_type=MESH,
        )
        copy.start()
        copies.append(copy)
        return copy

    def share(ref, device):
        return send(ref, ref, device)

    def slot(v):
        return gath.at[pl.ds(pl.multiple_of(16 * v, 16), 16), :]

    p4, p2, p1 = at_zl(flip(zl, 4)), at_zl(flip(zl, 2)), at_zl(flip(zl, 1))
    s4 = share(slot(q), p4)
    s2 = share(slot(q), p2)
    s1 = [share(slot(q), p1)]
    s4.wait_recv()
    s24 = share(slot(flip(q, 1)), p2)
    s1.append(share(slot(flip(q, 1)), p1))
    s2.wait_recv()
    s1.append(share(slot(flip(q, 2)), p1))
    s24.wait_recv()
    s1.append(share(slot(flip(flip(q, 2), 1)), p1))
    for copy in s1:
        copy.wait_recv()

    rows = dot(pick, gath[...], 1, 0).astype(BF)
    for t, unit in enumerate((0, 1, 11)):
        xc[unit, c] = rows[32 * t : 32 * t + 32]

    def u(unit):
        return xc.at[unit, c]

    def two(unit):
        return xc.at[pl.ds(unit, 2), c]

    def half(unit, at):
        return xc.at[unit, c, pl.ds(at, 16), :]

    r0, l0 = send(u(0), u(2), at_x(1)), send(u(0), u(3), at_x(3))
    k0 = share(two(0), core)
    r1, l1 = send(u(1), u(4), at_x(1)), send(u(1), u(5), at_x(3))
    r0.wait_recv()
    l0.wait_recv()
    k1 = share(two(2), core)
    rr0 = send(u(2), u(6), at_x(1))
    r2, l2 = send(u(11), u(8), at_x(1)), send(u(11), u(9), at_x(3))
    r1.wait_recv()
    rr1 = send(half(4, 0), half(7, 0), at_x(1))
    l1.wait_recv()
    ll1 = send(half(5, 16), half(7, 16), at_x(3))
    k2 = share(two(4), core)

    def piece(ref, k, t, at, n):
        return ref.at[k, t, pl.ds(pl.multiple_of(n * at, n), n), :]

    def scatter_a(k, srcb, n, pos, to, recv):
        l1 = send(piece(srcb, k, 0, mod(pos + 2, 4), n), recv.at[k, 0], to(3))
        r1 = send(piece(srcb, k, 1, mod(pos + 2, 4), n), recv.at[k, 1], to(1))
        l2 = send(piece(srcb, k, 1, mod(pos - 1, 4), n), recv.at[k, 2], to(3))
        r2 = send(piece(srcb, k, 0, mod(pos + 1, 4), n), recv.at[k, 3], to(1))
        return l1, r1, l2, r2

    def scatter_b(k, srcf, n, pos, to, recv, last, tmp, first):
        l1, r1, _, _ = first
        l1.wait_recv()
        tmp[k, 0] = (piece(srcf, k, 0, mod(pos - 1, 4), n)[...] + recv[k, 0].astype(F32)).astype(tmp.dtype)
        l3 = send(tmp.at[k, 0], last.at[k, 0], to(3))
        r1.wait_recv()
        tmp[k, 1] = (piece(srcf, k, 1, mod(pos + 1, 4), n)[...] + recv[k, 1].astype(F32)).astype(tmp.dtype)
        r3 = send(tmp.at[k, 1], last.at[k, 1], to(1))
        return l3, r3

    def scatter_c(k, srcf, n, pos, recv, last, first, second):
        _, _, l2, r2 = first
        l3, r3 = second
        r2.wait_recv()
        l3.wait_recv()
        a = piece(srcf, k, 0, pos, n)[...] + recv[k, 3].astype(F32) + last[k, 0].astype(F32)
        l2.wait_recv()
        r3.wait_recv()
        b = piece(srcf, k, 1, pos, n)[...] + recv[k, 2].astype(F32) + last[k, 1].astype(F32)
        return a, b

    def rows_of(base, at, n):
        return pl.ds(pl.multiple_of(base + n * at, n), n)

    def gather_a(k, t, base, n, pos, to):
        own = hg.at[k, t, rows_of(base, pos, n), :]
        return share(own, to(1)), share(own, to(3))

    ya, yb, za, zb, cs = ([None] * NK for _ in range(5))
    ga, gb, fa, fb = ([[None] * 2 for _ in range(NK)] for _ in range(4))

    def tokens(k, t):
        return xc[4 * k : 4 * k + 4, :, :, W * t : W * t + W].reshape(ROWS, W)

    def products(k):
        for t, (w, dim) in enumerate(((w1_ref, 0), (w2_ref, 1))):
            a = dot(tokens(k, t), w[...], 1, dim)
            pf[k, t] = a
            pb[k, t] = a.astype(BF)

    def y_first(k):
        ya[k] = scatter_a(k, pb, YR, y, at_y, ry)

    def y_second(k):
        yb[k] = scatter_b(k, pf, YR, y, at_y, ry, ry3 if k else ry0, ty if k else ty0, ya[k])

    def z_first(k):
        a, b = scatter_c(k, pf, YR, y, ry, ry3 if k else ry0, ya[k], yb[k])
        sf[k, 0], sf[k, 1] = a, b
        sb[k, 0], sb[k, 1] = a.astype(BF), b.astype(BF)
        za[k] = scatter_a(k, sb, ZR, zh, at_zh, rz.at[:, 0:4])

    def z_second(k):
        zb[k] = scatter_b(k, sf, ZR, zh, at_zh, rz, rz.at[:, 4:6], tz, za[k])

    def z_back(k):
        pre, grad = scatter_c(k, sf, ZR, zh, rz, rz.at[:, 4:6], za[k], zb[k])
        cdf = 0.5 * (1.0 + lax.erf(pre * math.sqrt(0.5)))
        pdf = jnp.exp(-0.5 * pre * pre) * (1.0 / math.sqrt(2.0 * math.pi))
        own = rows_of(YR * y, zh, ZR)
        hg[k, 0, own, :] = (pre * cdf).astype(BF)
        hg[k, 1, own, :] = (grad * (cdf + pre * pdf)).astype(BF)
        z_own(k, 1)

    def z_own(k, t):
        ga[k][t] = gather_a(k, t, YR * y, ZR, zh, at_zh)

    def z_relay(k, t):
        r, l = ga[k][t]
        if (k + t) % 2:
            r.wait_recv()
            gb[k][t] = share(hg.at[k, t, rows_of(YR * y, mod(zh - 1, 4), ZR), :], at_zh(1)), l
        else:
            l.wait_recv()
            gb[k][t] = share(hg.at[k, t, rows_of(YR * y, mod(zh + 1, 4), ZR), :], at_zh(3)), r

    def y_back(k, t):
        for copy in gb[k][t]:
            copy.wait_recv()
        fa[k][t] = gather_a(k, t, 0, YR, y, at_y)

    def y_direct(k, t):
        for copy in gb[k][t]:
            copy.wait_recv()
        own = hg.at[k, t, rows_of(0, y, YR), :]
        fb[k][t] = [share(own, at_y(d)) for d in (2, 1, 3)]

    def y_relay(k, t):
        r, l = fa[k][t]
        r.wait_recv()
        r2 = share(hg.at[k, t, rows_of(YR * mod(y - 1, 4), 0, 32), :], at_y(1))
        l.wait_recv()
        l2 = share(hg.at[k, t, rows_of(YR * mod(y + 1, 4) + 32, 0, 32), :], at_y(3))
        fb[k][t] = r2, l2

    def back_core(k):
        for copy in fb[k][1]:
            copy.wait_recv()
        rf[k] = dot(hg[k, 1], w1_ref[...], 1, 1).reshape(4, 2, 32, W)
        cs[k] = send(rf.at[k, :, 1 - c], rc.at[k], core)

    def back_sum(k):
        cs[k].wait_recv()
        for u in range(4):
            rf[k, u, c] = rf[k, u, c] + rc[k, u]

    def back_x(k, unit, n, at, side):
        return send(rf.at[k, pl.ds(unit, n), c], rx.at[side, pl.ds(at, n)], at_x((3, 1, 2)[side]))

    def back_x_short(slot, k, unit, side):
        xs2[slot] = rf[k, unit, c].astype(BF)
        return send(xs2.at[slot], rx2.at[slot], at_x((3, 1, 2)[side]))

    def add(ref, k, value):
        if k == 0:
            ref[...] = value
        else:
            ref[...] += value

    def grad_up(k):
        add(gu_ref, k, dot(tokens(k, 0), hg[k, 1], 0, 0))

    def grad_down(k):
        for copy in fb[k][0]:
            copy.wait_recv()
        add(gd_ref, k, dot(hg[k, 0], tokens(k, 1), 0, 0))

    k0.wait_recv()
    k1.wait_recv()
    loads[2].wait()
    loads[3].wait()
    products(0)
    y_first(0)
    l2.wait_recv()
    ll2 = send(u(9), u(10), at_x(3))
    r2.wait_recv()
    k4 = share(two(8), core)
    k5 = share(u(11), core)
    for copy in (rr0, rr1, ll1):
        copy.wait_recv()
    k3 = share(two(6), core)
    y_second(0)
    k2.wait_recv()
    k3.wait_recv()
    products(1)
    y_first(1)
    ll2.wait_recv()
    k6 = share(u(10), core)
    z_first(0)
    for copy in (k4, k5, k6):
        copy.wait_recv()
    products(2)
    y_second(1)
    y_first(2)
    z_first(1)
    y_second(2)
    z_second(0)
    z_first(2)
    z_second(1)
    z_back(0)
    z_second(2)
    z_back(1)
    z_relay(0, 1)
    z_back(2)
    z_relay(1, 1)
    z_own(0, 0)
    y_back(0, 1)
    z_relay(2, 1)
    z_own(1, 0)
    y_relay(0, 1)
    y_back(1, 1)
    z_own(2, 0)
    back_core(0)
    z_relay(0, 0)
    y_relay(1, 1)
    back_sum(0)
    xs = [back_x(0, 2, 1, 0, 0), back_x(0, 3, 1, 0, 1)]
    y_direct(2, 1)
    back_core(1)
    grad_up(0)
    back_sum(1)
    xs += [back_x_short(3, 1, 2, 2), back_x_short(4, 1, 3, 2), back_x(1, 0, 1, 1, 0), back_x(1, 1, 1, 1, 1)]
    z_relay(1, 0)
    z_relay(2, 0)
    back_core(2)
    y_back(0, 0)
    grad_up(1)
    back_sum(2)
    last = [back_x_short(side, 2, unit, side) for side, unit in ((2, 2), (0, 0), (1, 1))]

    def over_zl(parts, spread, n, held, recv):
        for l in range(3):
            for t, part in enumerate(parts):
                at = 32 * (len(parts) * l + t)
                zin[at : at + 32, :] = part[:, 128 * l : 128 * l + 128].astype(BF)
        used = 96 * len(parts)
        held[...] = dot(spread, zin[0:used, :], 0, 0).astype(BF)
        done = []
        for d in (4, 3, 5, 2, 6, 1, 7):
            to = lax.rem(zl + d, 8)
            done.append(send(held.at[pl.ds(pl.multiple_of(n * rev3(to), n), n), :], recv.at[d - 1], at_zl(to)))
        return done

    def over_zl_sum(n, held, recv):
        total = held[pl.ds(pl.multiple_of(n * q, n), n), :].astype(F32)
        for d in range(7):
            total += recv[d].astype(F32)
        return total

    for copy in xs:
        copy.wait_recv()
    early = over_zl([rf[0, t, c] + rx[0, t] + rx[1, t] + rx2[3 + t].astype(F32) for t in range(2)], pick2, 32, zs, rzz)
    y_relay(0, 0)
    y_back(1, 0)
    grad_up(2)
    stores = [pltpu.make_async_copy(gu_ref, gu_hbm, store_sem.at[0])]
    stores[0].start()
    for copy in last:
        copy.wait_recv()
    own = rf[2, 3, c]
    for side in range(3):
        own += rx2[side].astype(F32)
    late = over_zl([own], pick, 16, zs2, rzz2)
    y_direct(2, 0)
    y_relay(1, 0)
    grad_down(0)
    grad_down(1)
    grad_down(2)
    stores.append(pltpu.make_async_copy(gd_ref, gd_hbm, store_sem.at[1]))
    stores[1].start()
    for copy in early:
        copy.wait_recv()
    total = over_zl_sum(32, zs, rzz)
    for copy in late:
        copy.wait_recv()
    total2 = over_zl_sum(16, zs2, rzz2).astype(BF)
    i = lax.broadcasted_iota(jnp.int32, (16, 16), 0)
    j = lax.broadcasted_iota(jnp.int32, (16, 16), 1)
    for l in range(3):
        back = jnp.where((i < 4) & (j == i + 4 * l), 1.0, 0.0).astype(BF)
        columns = slice(128 * l, 128 * l + 128)
        gi_ref[0:8, columns] = total[8 * l : 8 * l + 8].astype(BF)
        gi_ref[8:12, columns] = dot(back, total2, 1, 0)[0:4].astype(BF)

    for store in stores:
        store.wait()
    for copy in copies:
        copy.wait_send()


def move(a, b, c, to_a, to_b, to_c, held_a, held_b, held_c, sem):
    moves = ((b, held_b, to_b), (c, held_c, to_c), (a, held_a, to_a))
    into = [pltpu.make_async_copy(src, held, sem.at[n]) for n, (src, held, _) in enumerate(moves)]
    out = [pltpu.make_async_copy(held, dst, sem.at[3 + n]) for n, (_, held, dst) in enumerate(moves)]
    for copy in into:
        copy.start()
    for first, second in zip(into, out):
        first.wait()
        second.start()
    for copy in out:
        copy.wait()


def body(inputs, cotangent, up_weight, down_weight):
    vmem = pl.BlockSpec(memory_space=pltpu.VMEM)
    hbm = pl.BlockSpec(memory_space=pltpu.HBM)
    results = pl.pallas_call(
        kernel,
        out_shape=(
            jax.ShapeDtypeStruct((12, W), BF),
            jax.ShapeDtypeStruct((W, W), F32),
            jax.ShapeDtypeStruct((W, W), F32),
        ),
        in_specs=[hbm] * 4,
        out_specs=(vmem, hbm, hbm),
        scratch_shapes=[
            pltpu.VMEM((W, W), F32),
            pltpu.VMEM((W, W), F32),
            pltpu.VMEM((2, 12, W), BF),
            pltpu.VMEM((W, W), BF),
            pltpu.VMEM((W, W), BF),
            pltpu.VMEM((128, 2 * W), BF),
            pltpu.VMEM((12, 2, 32, 2 * W), BF),
            pltpu.VMEM((NK, 2, ROWS, W), F32),
            pltpu.VMEM((NK, 2, ROWS, W), BF),
            pltpu.VMEM((NK, 4, YR, W), BF),
            pltpu.VMEM((NK, 2, YR, W), F32),
            pltpu.VMEM((NK, 2, YR, W), F32),
            pltpu.VMEM((1, 2, YR, W), BF),
            pltpu.VMEM((1, 2, YR, W), BF),
            pltpu.VMEM((NK, 2, YR, W), F32),
            pltpu.VMEM((NK, 2, YR, W), BF),
            pltpu.VMEM((NK, 6, ZR, W), BF),
            pltpu.VMEM((NK, 2, ZR, W), BF),
            pltpu.VMEM((NK, 2, ROWS, W), BF),
            pltpu.VMEM((NK, 4, 2, 32, W), F32),
            pltpu.VMEM((NK, 4, 32, W), F32),
            pltpu.VMEM((2, 2, 32, W), F32),
            pltpu.VMEM((5, 32, W), BF),
            pltpu.VMEM((5, 32, W), BF),
            pltpu.VMEM((192, 128), BF),
            pltpu.VMEM((256, 128), BF),
            pltpu.VMEM((7, 32, 128), BF),
            pltpu.VMEM((128, 128), BF),
            pltpu.VMEM((7, 16, 128), BF),
            pltpu.SemaphoreType.DMA((4,)),
            pltpu.SemaphoreType.DMA((2,)),
            pltpu.SemaphoreType.DMA((COPIES,)),
            pltpu.SemaphoreType.DMA((COPIES,)),
        ],
        compiler_params=pltpu.CompilerParams(
            collective_id=0, has_side_effects=True, vmem_limit_bytes=56 * 1024 * 1024
        ),
        name="mlp_backward",
    )(inputs, cotangent, up_weight, down_weight)
    return pl.pallas_call(
        move,
        out_shape=tuple(jax.ShapeDtypeStruct(r.shape, r.dtype) for r in results),
        in_specs=[hbm] * 3,
        out_specs=(hbm,) * 3,
        scratch_shapes=[pltpu.VMEM(r.shape, r.dtype) for r in results] + [pltpu.SemaphoreType.DMA((6,))],
        compiler_params=pltpu.CompilerParams(vmem_limit_bytes=56 * 1024 * 1024),
        name="move_results",
    )(*results)


def solution(mesh):
    placed = (
        P(("gx", "gz"), "gy"),
        P(("gx", "gz"), "gy"),
        P("gy", ("gz", "gx")),
        P(("gz", "gx"), "gy"),
    )
    return jax.shard_map(
        body,
        mesh=mesh,
        in_specs=placed,
        out_specs=(P(("gx", "gz"), "gy"), P("gy", ("gz", "gx")), P(("gz", "gx"), "gy")),
        check_vma=False,
    )
```
